512 devices in a mesh: grp: 16 (over z, core), own: 32 (over x, y).
Axes of the slice: x: 4, y: 8, z: 8, core: 2. Of those that a mesh axis runs over, the one named last changes fastest.
Arguments:
- sensitivity: bfloat16 [131072, 64, 128], P(('grp', 'own')), may hold values from -0.75 to 0.75
- residual: bfloat16 [16384, 64], P(('grp', 'own')), may hold values from -6 to 6
- conductivity: float32 [128, 256, 128], P('grp', 'own'), may hold values from -6 to 6
- along_first: float32 [128, 256, 128], P('grp', 'own'), may hold values from 0.3 to 3
- along_second: float32 [128, 256, 128], P('grp', 'own'), may hold values from 0.3 to 3
- along_depth: float32 [128, 256, 128], P('grp', 'own'), may hold values from 0.3 to 3
- sounding: int32 [131072], P(('grp', 'own')), may hold values from 0 to 31
- owner: int32 [131072, 1], P(('grp', 'own')), may hold values from 0 to 31; in each aligned block of 256 rows (0 to 255, 256 to 511, ...) at most 16 rows name the same one
- column: int32 [131072], P(('grp', 'own')), may hold values from 0 to 63
- live_count: int32 [512], P(('grp', 'own')), may hold values from 64 to 256, as said below
Outputs:
- gradient: float32 [128, 256, 128], P('grp', 'own')
The draws below stay inside these ranges and needn't reach their ends.
Inputs may be any that keep to these rules, and one draw needn't show every extreme that they name: Among the 256 blocks of one device no owner index appears more than 16 times, and in every draw some device has an owner index exactly 16 times. `live_count`: some device has all its 256 blocks live in every draw.
All inputs are finite; a program needn't handle non-finite values.
Results may differ from the reference program's by a relative error of at most 0.0003.
Values sent between devices are 32-bit elements; how exact they have to be, the bound alone decides.
A program may use at most 64 MiB of HBM per device.

```python
import math
import jax
import jax.numpy as jnp
import numpy as np
from jax import lax

ND = 64
NZ = 128
CX = 8
CY = 8
BLK_DEV = 256
SND_DEV = 32
CAP = 16
NDEV = 512
NBLK = 131072
NSND = 16384
COLS_DEV = 64
NX = 128
NY = 256
N_OWN = 32


def draw_live_count(key, part):
    counts = jax.random.randint(key, (NDEV,), BLK_DEV // 4, BLK_DEV + 1)
    fullest = jax.random.randint(jax.random.fold_in(key, 7), (), 0, NDEV)
    return counts.at[fullest].set(BLK_DEV).astype(jnp.int32)


def touch_ends(values, key, least, high):
    spot = [jax.random.randint(jax.random.fold_in(key, axis), (), 0, length) for axis, length in enumerate(values.shape)]
    longest = values.shape.index(max(values.shape))
    next_to = spot[:longest] + [(spot[longest] + 1) % values.shape[longest]] + spot[longest + 1:]
    return values.at[tuple(spot)].set(least).at[tuple(next_to)].set(high)


def level_of(rng, extent, split, least, largest):
    def one(dim, blocks):
        heights = jax.random.uniform(jax.random.fold_in(jax.random.fold_in(rng, 6), dim), (blocks,), jnp.float32, least / len(split), largest / len(split))
        return jnp.repeat(jnp.exp(heights), extent[dim] // blocks).reshape((-1,) + (1,) * (len(extent) - dim - 1))

    gain = one(*split[0])
    for cut in split[1:]:
        gain = gain * one(*cut)
    return gain


def shared_out(own_key, own, number, rows, number_of, top, limit, skew):
    sequence = jax.random.permutation(own_key, number_of)
    crowded, ordinary = load_shares(number_of, rows * top, limit, skew, True), load_shares(number_of, rows * top, limit, skew, False)
    places = jnp.arange(number_of)

    def named(lengths, turn):
        used = int((lengths > 0).sum())
        fixed = max(1, used // 4)
        shifted = fixed + (places - fixed + turn * (used - fixed)) % max(1, number_of - fixed)
        return jnp.zeros((number_of,), jnp.int32).at[sequence[jnp.where(places < fixed, places, shifted)]].set(jnp.asarray(lengths, jnp.int32))

    lengths = jnp.where(number % 4 == 0, named(crowded, number // 4), named(ordinary, number - number // 4 - 1))
    mixed = jax.random.permutation(jax.random.fold_in(own, 3), number_of)
    source_of, receiver = mixed[0:number_of // 2 * 2:2], mixed[1:number_of // 2 * 2:2]
    slack = jnp.minimum(lengths[source_of] - 1, limit - lengths[receiver]) // 2
    slack = jnp.where((source_of == sequence[0]) | (receiver == sequence[0]) | (lengths[receiver] == 0), 0, jnp.maximum(slack, 0))
    shifted = jax.random.randint(jax.random.fold_in(own, 4), (number_of // 2,), 0, 1 << 20) % (slack + 1)
    lengths = lengths.at[source_of].add(-shifted).at[receiver].add(shifted)
    items = jnp.searchsorted(jnp.cumsum(lengths), jnp.arange(rows * top), side="right").astype(jnp.int32)
    grid = items.reshape(top, rows).T
    grid = grid[jax.random.permutation(jax.random.fold_in(own, 1), rows)]
    turn = jax.random.randint(jax.random.fold_in(own, 2), (rows, 1), 0, top)
    return jnp.take_along_axis(grid, (jnp.arange(top)[None, :] + turn) % top, axis=1)


def load_shares(number_of, total, most, lean, full):
    portions = [(1 << 20) // math.isqrt(grade ** lean) + 1 for grade in range(1, number_of + 1)]
    largest = most if full else min(most, max(-(-total // number_of), total * portions[0] // sum(portions)))
    least = 1 if total - largest >= number_of - 1 else 0
    given, surplus = [largest] + [least] * (number_of - 1), total - largest - least * (number_of - 1)
    while surplus > 0:
        movable = [i for i in range(1, number_of) if given[i] < largest] or [i for i in range(1, number_of) if given[i] < most]
        mass, budget = sum([portions[i] for i in movable]), surplus
        for i in movable:
            addition = min(most - given[i], max(1, budget * portions[i] // mass), surplus)
            given[i] = given[i] + addition
            surplus = surplus - addition
    return np.array(given)


def centred(stream_key, extent, scale, most, cuts=(), kind=jnp.bfloat16):
    factor_of = level_of(stream_key, extent, cuts, -0.22, 0.18) if cuts else 1.0
    values = jax.random.normal(stream_key, extent, jnp.float32) * scale * factor_of
    return jnp.minimum(jnp.maximum(values, -most), most).astype(kind)


def setup_inputs(seed: int = 0) -> dict:
    key_of = jax.random.split(jax.random.key(seed), 11)
    sensitivity = centred(key_of[0], (NBLK, ND, NZ), ND ** -0.5, 0.75, ((0, 512),))
    residual = centred(key_of[1], (NSND, ND), 1.0, 6.0, ((0, 512),))
    conductivity = centred(key_of[2], (NX, NY, NZ), 1.0, 6.0, ((0, 16), (1, 32)), jnp.float32)
    along_first = jnp.clip(jnp.exp(math.log(3.0) - 2.3025851 * jax.random.uniform(key_of[3], (NX, NY, NZ), jnp.float32) ** level_of(key_of[3], (NX, NY, NZ), ((0, 16), (1, 32)), -0.2, 0.2)), 0.3, 3.0)
    along_second = jnp.clip(jnp.exp(math.log(3.0) - 2.3025851 * jax.random.uniform(key_of[4], (NX, NY, NZ), jnp.float32) ** level_of(key_of[4], (NX, NY, NZ), ((0, 16), (1, 32)), -0.2, 0.2)), 0.3, 3.0)
    along_depth = jnp.clip(jnp.exp(math.log(3.0) - 2.3025851 * jax.random.uniform(key_of[5], (NX, NY, NZ), jnp.float32) ** level_of(key_of[5], (NX, NY, NZ), ((0, 16), (1, 32)), -0.2, 0.2)), 0.3, 3.0)
    sounding = touch_ends(jax.random.randint(key_of[6], (NBLK,), 0, SND_DEV), jax.random.fold_in(key_of[6], 1), 0, SND_DEV - 1).astype(jnp.int32)
    owner_keys = jax.random.split(jax.random.fold_in(key_of[7], 1), NBLK // BLK_DEV)
    owner_turns = jax.random.permutation(jax.random.fold_in(key_of[7], 3), NBLK // BLK_DEV)
    owner = jax.vmap(lambda own, number: shared_out(jax.random.fold_in(key_of[7], 2), own, number, BLK_DEV, N_OWN, 1, CAP, 2))(owner_keys, owner_turns).reshape((NBLK, 1))
    column = touch_ends(jax.random.randint(key_of[8], (NBLK,), 0, COLS_DEV), jax.random.fold_in(key_of[8], 1), 0, COLS_DEV - 1).astype(jnp.int32)
    live_count = draw_live_count(jax.random.fold_in(key_of[10], 71), 0)
    return {"sensitivity": sensitivity, "residual": residual, "conductivity": conductivity, "along_first": along_first, "along_second": along_second, "along_depth": along_depth, "sounding": sounding, "owner": owner, "column": column, "live_count": live_count}


def smooth_part(field, weights, axis):
    size = field.shape[axis]
    upper = jnp.concatenate([lax.slice_in_dim(field, 1, size, axis=axis), lax.slice_in_dim(field, size - 1, size, axis=axis)], axis)
    flux = weights * (upper - field)
    earlier = jnp.concatenate([jnp.zeros_like(lax.slice_in_dim(flux, 0, 1, axis=axis)), lax.slice_in_dim(flux, 0, size - 1, axis=axis)], axis)
    return earlier - flux


def reference(sensitivity, residual, conductivity, along_first, along_second, along_depth, sounding, owner, column, live_count):
    blocks4 = sensitivity.reshape(NDEV, BLK_DEV, ND, NZ)
    rows3 = residual.reshape(NDEV, SND_DEV, ND)
    index2 = sounding.reshape(NDEV, BLK_DEV)

    def device_terms(item):
        blocks, rows, picks, count = item
        chosen = jnp.take(rows, picks, axis=0).astype(jnp.float32)
        terms = jnp.einsum('bij,bi->bj', blocks.astype(jnp.float32), chosen)
        keep = jnp.arange(BLK_DEV, dtype=jnp.int32) < count
        return jnp.where(keep[:, None], terms, jnp.zeros_like(terms))

    terms = lax.map(device_terms, (blocks4, rows3, index2, live_count))
    device = jnp.arange(NBLK, dtype=jnp.int32) // BLK_DEV
    group = device // N_OWN
    first = group * CX + column.astype(jnp.int32) // CY
    second = owner[:, 0].astype(jnp.int32) * CY + column.astype(jnp.int32) % CY
    flat = (first * NY + second).astype(jnp.int32)
    data_part = jnp.zeros((NX * NY, NZ), jnp.float32).at[flat].add(terms.reshape(NBLK, NZ)).reshape(NX, NY, NZ)
    smooth = smooth_part(conductivity, along_first, 0) + smooth_part(conductivity, along_second, 1)
    smooth = smooth + smooth_part(conductivity, along_depth, 2)
    return data_part + smooth
```

```python
import functools

import jax
import jax.numpy as jnp
from jax import lax
from jax.experimental import pallas as pl
from jax.experimental.pallas import tpu as pltpu
from jax.sharding import PartitionSpec as P

MESH = pl.DeviceIdType.MESH
CAP = 16
F32 = jnp.float32
BF16 = jnp.bfloat16


def iota(shape, dim):
    return lax.broadcasted_iota(jnp.int32, shape, dim)


def far_first(count):
    return sorted(range(count), key=lambda d: (-min(d, count - d), d))


def split(values):
    high = values.astype(BF16)
    low = (values - high.astype(F32)).astype(BF16)
    return jnp.concatenate([high, low], axis=-1)


def kernel(
    groups,
    xs,
    ys,
    chunks,
    sens_hbm,
    res_hbm,
    model_hbm,
    first_hbm,
    second_hbm,
    depth_hbm,
    sounding_hbm,
    owner_hbm,
    column_hbm,
    live_hbm,
    out_ref,
    sens,
    res,
    field,
    index,
    live,
    terms,
    packed,
    landed,
    tags,
    tags_in,
    halo_first,
    halo_second,
    sens_sem,
    in_sem,
    send_sem,
    recv_sem,
    tag_sem,
    halo_send,
    halo_recv,
):
    owners = xs * ys
    g = lax.axis_index("grp")
    o = lax.axis_index("own")
    x, y = o // ys, o % ys
    blocks = index.shape[2]
    nd = sens.shape[0] // blocks
    lanes = sens.shape[1]
    order = far_first(ys)

    small = [
        pltpu.make_async_copy(owner_hbm, index.at[0], in_sem.at[0]),
        pltpu.make_async_copy(column_hbm, index.at[1], in_sem.at[1]),
        pltpu.make_async_copy(sounding_hbm, index.at[2], in_sem.at[2]),
        pltpu.make_async_copy(live_hbm, live, in_sem.at[3]),
        pltpu.make_async_copy(res_hbm, res, in_sem.at[4]),
    ]
    for copy in small:
        copy.start()
    rows = sens.shape[0] // chunks
    big = [
        pltpu.make_async_copy(
            sens_hbm.at[pl.ds(c * rows, rows)], sens.at[pl.ds(c * rows, rows)], sens_sem.at[c]
        )
        for c in range(chunks)
    ]
    for copy in big:
        copy.start()
    mesh_in = [
        pltpu.make_async_copy(src, field.at[k], in_sem.at[5 + k])
        for k, src in enumerate((model_hbm, first_hbm, second_hbm, depth_hbm))
    ]
    for copy in mesh_in:
        copy.start()

    barrier = pltpu.get_barrier_semaphore()
    around = [
        {"grp": lax.rem(g + 1, groups)},
        {"grp": lax.rem(g + groups - 1, groups)},
    ]
    peers = [None] * owners
    for p in range(ys):
        for dx in range(xs):
            r = p * xs + dx
            peers[r] = {"own": lax.rem(x + dx, xs) * ys + lax.rem(y + order[p], ys)}
    self_slot = order.index(0) * xs
    others = [r for r in range(owners) if r != self_slot]
    for device in around + [peers[r] for r in others]:
        pl.semaphore_signal(barrier, inc=1, device_id=device, device_id_type=MESH)

    for copy in small[:4]:
        copy.wait()
    owner = index[0]
    column = index[1]
    sounding = index[2]
    delta_x = lax.rem(owner // ys - x + xs, xs)
    delta_y = lax.rem(owner % ys - y + ys, ys)
    place = jnp.zeros_like(owner)
    for p in range(ys):
        place = jnp.where(delta_y == order[p], p, place)
    target = place * xs + delta_x
    hot = jnp.where(iota((owners, blocks), 0) == target, 1.0, 0.0)
    before = jnp.where(iota((blocks, blocks), 0) < iota((blocks, blocks), 1), 1.0, 0.0)
    earlier = jnp.dot(hot.astype(BF16), before.astype(BF16), preferred_element_type=F32)
    rank = jnp.sum(hot * earlier, axis=0, keepdims=True).astype(jnp.int32)
    slot = target * CAP + rank

    value = jnp.where(
        lax.rem(iota((lanes, blocks), 0), CAP) == rank, column.astype(F32), 0.0
    )
    tag = lax.dot_general(
        hot.astype(BF16),
        value.astype(BF16),
        (((1,), (1,)), ((), ())),
        preferred_element_type=F32,
    )
    per_row = lanes // CAP
    mine = iota((owners, lanes), 1) // CAP == lax.rem(iota((owners, lanes), 0), per_row)
    tag = jnp.where(mine, tag, 0.0)
    for r in range(owners):
        tags[r] = tag[r : r + 1]
    tags_in[self_slot] = tag[self_slot : self_slot + 1]

    pl.semaphore_wait(barrier, len(around) + len(others))

    halo = []
    for k, (src, dst, device) in enumerate(
        (
            (model_hbm.at[field.shape[1] - 1], halo_first.at[0], around[0]),
            (first_hbm.at[field.shape[1] - 1], halo_first.at[1], around[0]),
            (model_hbm.at[0], halo_first.at[2], around[1]),
            (
                model_hbm.at[:, pl.ds(field.shape[2] - 1, 1)],
                halo_second.at[0],
                {"own": lax.rem(o + 1, owners)},
            ),
            (
                second_hbm.at[:, pl.ds(field.shape[2] - 1, 1)],
                halo_second.at[1],
                {"own": lax.rem(o + 1, owners)},
            ),
            (
                model_hbm.at[:, pl.ds(0, 1)],
                halo_second.at[2],
                {"own": lax.rem(o + owners - 1, owners)},
            ),
        )
    ):
        halo.append(
            pltpu.make_async_remote_copy(
                src_ref=src,
                dst_ref=dst,
                send_sem=halo_send.at[k],
                recv_sem=halo_recv.at[k],
                device_id=device,
                device_id_type=MESH,
            )
        )
    for copy in halo:
        copy.start()

    def tag_copy(first, count, device):
        return pltpu.make_async_remote_copy(
            src_ref=tags.at[pl.ds(first, count)],
            dst_ref=tags_in.at[pl.ds(first, count)],
            send_sem=tag_sem.at[0],
            recv_sem=tag_sem.at[1],
            device_id=device,
            device_id_type=MESH,
        )

    for r in others:
        tag_copy(r, 1, peers[r]).start()

    small[4].wait()
    keep = iota((1, blocks), 1) < live[0]
    picked = jnp.where(
        (iota((res.shape[0], blocks), 0) == sounding) & keep, 1.0, 0.0
    ).astype(BF16)
    twice = jnp.concatenate([res[...]] * (lanes // nd), axis=1)
    chosen = lax.dot_general(
        picked, twice, (((0,), (0,)), ((), ())), preferred_element_type=F32
    ).astype(BF16)
    at_once = 16
    wide = at_once * nd
    diagonal = jnp.where(
        iota((at_once, wide), 0) == iota((at_once, wide), 1) // nd, 1.0, 0.0
    ).astype(BF16)
    done = 0
    for b in range(0, blocks, at_once):
        while done * rows < (b + at_once) * nd:
            big[done].wait()
            done += 1
        left = jnp.concatenate([chosen[b : b + at_once]] * (wide // lanes), axis=1) * diagonal
        part = jnp.dot(left, sens[pl.ds(b * nd, wide)], preferred_element_type=F32)
        terms[pl.ds(b, at_once)] = split(part)

    def packet(first, count, group, device):
        return pltpu.make_async_remote_copy(
            src_ref=packed.at[pl.ds(first, count)],
            dst_ref=landed.at[pl.ds(first, count)],
            send_sem=send_sem.at[0],
            recv_sem=recv_sem.at[group],
            device_id=device,
            device_id_type=MESH,
        )

    step = 2
    for p in range(0, ys, step):
        count = step * xs * CAP
        chosen_rows = jnp.where(
            iota((count, blocks), 0) + p * xs * CAP == slot, 1.0, 0.0
        ).astype(BF16)
        both = jnp.dot(chosen_rows, terms[...], preferred_element_type=F32)
        sums = (both[:, :lanes] + both[:, lanes:]).reshape(step * xs, CAP, lanes)
        packed[pl.ds(p * xs, step * xs)] = sums
        for r in range(p * xs, (p + step) * xs):
            if r != self_slot:
                packet(r, 1, r // xs, peers[r]).start()
            else:
                landed[r] = sums[r - p * xs]

    for copy in mesh_in:
        copy.wait()
    for copy in halo:
        copy.wait()
    model, w1, w2, w3 = field[0], field[1], field[2], field[3]
    cx, cy = field.shape[1], field.shape[2]
    shape = (cx, cy, lanes)

    above = jnp.concatenate([model[1:], halo_first[2][None]], axis=0)
    flux = w1 * (above - model)
    flux = jnp.where((iota(shape, 0) == cx - 1) & (g == groups - 1), 0.0, flux)
    behind = jnp.where(g == 0, 0.0, halo_first[1] * (model[0] - halo_first[0]))
    smooth = jnp.concatenate([behind[None], flux[:-1]], axis=0) - flux

    row = iota(shape, 1)
    above = jnp.where(row == cy - 1, halo_second[2], pltpu.roll(model, cy - 1, 1))
    flux = w2 * (above - model)
    flux = jnp.where((row == cy - 1) & (o == owners - 1), 0.0, flux)
    behind = halo_second[1] * (model[:, 0:1] - halo_second[0])
    behind = jnp.where(o == 0, 0.0, behind)
    smooth = smooth + (jnp.where(row == 0, behind, pltpu.roll(flux, 1, 1)) - flux)

    cell = iota(shape, 2)
    flux = jnp.where(cell == lanes - 1, 0.0, w3 * (pltpu.roll(model, lanes - 1, 2) - model))
    smooth = smooth + (jnp.where(cell == 0, 0.0, pltpu.roll(flux, 1, 2)) - flux)

    tag_copy(0, owners - 1, peers[others[0]]).wait_recv()
    cells = cx * cy
    total = jnp.zeros((cells, 2 * lanes), F32)
    half = owners // 2
    for h in range(2):
        for p in range(h * ys // 2, (h + 1) * ys // 2):
            first, count = p * xs, xs
            if p == self_slot // xs:
                first, count = first + 1, count - 1
            packet(first, count, p, peers[others[0]]).wait_recv()
        names = []
        for q in range(h * half, (h + 1) * half, per_row):
            name = tags_in[q]
            for r in range(q + 1, q + per_row):
                name = name + tags_in[r]
            names.append(name)
        name = jnp.concatenate(names, axis=1).astype(jnp.int32)
        hit = jnp.where(iota((cells, half * CAP), 0) == name, 1.0, 0.0).astype(BF16)
        got = landed[pl.ds(h * half, half)].reshape(half * CAP, lanes)
        total = total + jnp.dot(hit, split(got), preferred_element_type=F32)
    data = (total[:, :lanes] + total[:, lanes:]).reshape(shape)
    out_ref[...] = data + smooth

    tag_copy(0, owners - 1, peers[others[0]]).wait_send()
    packet(0, owners - 1, 0, peers[others[0]]).wait_send()


def solution(mesh):
    groups, owners = mesh.shape["grp"], mesh.shape["own"]
    xs = 4
    ys = owners // xs

    def per_device(sens, res, model, first, second, depth, sounding, owner, column, live):
        blocks, nd, lanes = sens.shape
        cx, cy, _ = model.shape
        chunks = 8
        hbm = pl.BlockSpec(memory_space=pltpu.HBM)
        return pl.pallas_call(
            functools.partial(kernel, groups, xs, ys, chunks),
            out_shape=jax.ShapeDtypeStruct(model.shape, F32),
            in_specs=[hbm] * 10,
            out_specs=pl.BlockSpec(memory_space=pltpu.VMEM),
            scratch_shapes=[
                pltpu.VMEM((blocks * nd, lanes), BF16),
                pltpu.VMEM(res.shape, BF16),
                pltpu.VMEM((4, cx, cy, lanes), F32),
                pltpu.VMEM((3, 1, blocks), jnp.int32),
                pltpu.SMEM((1,), jnp.int32),
                pltpu.VMEM((blocks, 2 * lanes), BF16),
                pltpu.VMEM((owners, CAP, lanes), F32),
                pltpu.VMEM((owners, CAP, lanes), F32),
                pltpu.VMEM((owners, 1, lanes), F32),
                pltpu.VMEM((owners, 1, lanes), F32),
                pltpu.VMEM((3, cy, lanes), F32),
                pltpu.VMEM((3, cx, 1, lanes), F32),
                pltpu.SemaphoreType.DMA((chunks,)),
                pltpu.SemaphoreType.DMA((9,)),
                pltpu.SemaphoreType.DMA((1,)),
                pltpu.SemaphoreType.DMA((ys,)),
                pltpu.SemaphoreType.DMA((2,)),
                pltpu.SemaphoreType.DMA((6,)),
                pltpu.SemaphoreType.DMA((6,)),
            ],
            compiler_params=pltpu.CompilerParams(
                collective_id=0, has_side_effects=True, vmem_limit_bytes=32 * 1024 * 1024
            ),
        )(
            sens.reshape(blocks * nd, lanes),
            res,
            model,
            first,
            second,
            depth,
            sounding.reshape(1, blocks),
            owner.reshape(1, blocks),
            column.reshape(1, blocks),
            live,
        )

    both = ("grp", "own")
    mesh_spec = P("grp", "own", None)
    return jax.shard_map(
        per_device,
        mesh=mesh,
        in_specs=(
            P(both, None, None),
            P(both, None),
            mesh_spec,
            mesh_spec,
            mesh_spec,
            mesh_spec,
            P(both),
            P(both, None),
            P(both),
            P(both),
        ),
        out_specs=mesh_spec,
        check_vma=False,
    )
```

```python
import functools

import jax
import jax.numpy as jnp
from jax import lax
from jax.experimental import pallas as pl
from jax.experimental.pallas import tpu as pltpu
from jax.sharding import PartitionSpec as P

MESH = pl.DeviceIdType.MESH
CAP = 16
F32 = jnp.float32
BF16 = jnp.bfloat16


def iota(shape, dim):
    return lax.broadcasted_iota(jnp.int32, shape, dim)


def rings(count):
    return sorted(range(count), key=lambda d: (min(d, count - d), d))


def split(values):
    high = values.astype(BF16)
    low = (values - high.astype(F32)).astype(BF16)
    return jnp.concatenate([high, low], axis=-1)


def kernel(
    groups,
    xs,
    ys,
    chunks,
    sens_hbm,
    res_hbm,
    model_hbm,
    first_hbm,
    second_hbm,
    depth_hbm,
    sounding_hbm,
    owner_hbm,
    column_hbm,
    live_hbm,
    out_ref,
    sens,
    res,
    field,
    index,
    live,
    terms,
    packed,
    landed,
    halo_first,
    halo_second,
    sens_sem,
    in_sem,
    send_sem,
    recv_sem,
    halo_send,
    halo_recv,
):
    owners = xs * ys
    g = lax.axis_index("grp")
    o = lax.axis_index("own")
    x, y = o // ys, o % ys
    blocks = index.shape[2]
    nd = sens.shape[0] // blocks
    lanes = sens.shape[1]
    order = rings(ys)
    far = y // (ys // 2 + 1)
    me = ((1 - far) * (2 * y - (y + ys - 1) // ys) + far * 2 * (ys - y)) * xs + x

    small = [
        pltpu.make_async_copy(owner_hbm, index.at[0], in_sem.at[0]),
        pltpu.make_async_copy(column_hbm, index.at[1], in_sem.at[1]),
        pltpu.make_async_copy(sounding_hbm, index.at[2], in_sem.at[2]),
        pltpu.make_async_copy(live_hbm, live, in_sem.at[3]),
        pltpu.make_async_copy(res_hbm, res, in_sem.at[4]),
    ]
    for copy in small:
        copy.start()
    rows = sens.shape[0] // chunks
    big = [
        pltpu.make_async_copy(
            sens_hbm.at[pl.ds(c * rows, rows)], sens.at[pl.ds(c * rows, rows)], sens_sem.at[c]
        )
        for c in range(chunks)
    ]
    for copy in big:
        copy.start()
    mesh_in = [
        pltpu.make_async_copy(src, field.at[k], in_sem.at[5 + k])
        for k, src in enumerate((model_hbm, first_hbm, second_hbm, depth_hbm))
    ]
    for copy in mesh_in:
        copy.start()

    peers = [{"own": (k % xs) * ys + order[k // xs]} for k in range(owners)]
    barrier = pltpu.get_barrier_semaphore()
    below, above = {"grp": g - 1}, {"grp": g + 1}

    def tell(semaphore, device):
        pl.semaphore_signal(semaphore, inc=1, device_id=device, device_id_type=MESH)

    for k in range(owners):
        pl.when(k != me)(functools.partial(tell, barrier, peers[k]))
    pl.when(g < groups - 1)(functools.partial(tell, barrier, above))
    pl.when(g > 0)(functools.partial(tell, barrier, below))

    for copy in small[:4]:
        copy.wait()
    owner = index[0]
    column = index[1]
    sounding = index[2]
    row = owner % ys
    row = jnp.where(row > ys // 2, 2 * (ys - row), jnp.maximum(2 * row - 1, 0))
    target = row * xs + owner // ys
    hot = jnp.where(iota((owners, blocks), 0) == target, 1.0, 0.0)
    before = jnp.where(iota((blocks, blocks), 0) < iota((blocks, blocks), 1), 1.0, 0.0)
    earlier = jnp.dot(hot.astype(BF16), before.astype(BF16), preferred_element_type=F32)
    rank = jnp.sum(hot * earlier, axis=0, keepdims=True).astype(jnp.int32)
    slot = target * CAP + rank

    value = jnp.where(
        lax.rem(iota((lanes, blocks), 0), CAP) == rank, column.astype(F32), 0.0
    )
    tag = lax.dot_general(
        hot.astype(BF16),
        value.astype(BF16),
        (((1,), (1,)), ((), ())),
        preferred_element_type=F32,
    )
    per_row = lanes // CAP
    tag = jnp.where(iota((owners, lanes), 1) // CAP == me % per_row, tag, 0.0)
    for k in range(owners):
        packed[k, CAP : CAP + 1] = tag[k : k + 1]

    small[4].wait()
    keep = iota((1, blocks), 1) < live[0]
    picked = jnp.where(
        (iota((res.shape[0], blocks), 0) == sounding) & keep, 1.0, 0.0
    ).astype(BF16)
    twice = jnp.concatenate([res[...]] * (lanes // nd), axis=1)
    chosen = lax.dot_general(
        picked, twice, (((0,), (0,)), ((), ())), preferred_element_type=F32
    ).astype(BF16)
    at_once = 16
    wide = at_once * nd
    diagonal = jnp.where(
        iota((at_once, wide), 0) == iota((at_once, wide), 1) // nd, 1.0, 0.0
    ).astype(BF16)
    done = 0
    for b in range(0, blocks, at_once):
        while done * rows < (b + at_once) * nd:
            big[done].wait()
            done += 1
        left = jnp.concatenate([chosen[b : b + at_once]] * (wide // lanes), axis=1) * diagonal
        part = jnp.dot(left, sens[pl.ds(b * nd, wide)], preferred_element_type=F32)
        terms[pl.ds(b, at_once)] = split(part)

    step = 2 * xs
    for k in range(0, owners, step):
        spots = jnp.where(
            iota((step * CAP, blocks), 0) + k * CAP == slot, 1.0, 0.0
        ).astype(BF16)
        both = jnp.dot(spots, terms[...], preferred_element_type=F32)
        sums = (both[:, :lanes] + both[:, lanes:]).reshape(step, CAP, lanes)
        packed[pl.ds(k, step), pl.ds(0, CAP)] = sums

    def packet(k, count=1):
        return pltpu.make_async_remote_copy(
            src_ref=packed.at[pl.ds(k, count), pl.ds(0, CAP + 1)],
            dst_ref=landed.at[pl.ds(me if count == 1 else k, count), pl.ds(0, CAP + 1)],
            send_sem=send_sem.at[0],
            recv_sem=recv_sem.at[me // per_row],
            device_id=peers[k],
            device_id_type=MESH,
        )

    cx, cy = field.shape[1], field.shape[2]

    def layer(n, src, dst, device):
        return pltpu.make_async_remote_copy(
            src_ref=src,
            dst_ref=dst,
            send_sem=halo_send.at[n],
            recv_sem=halo_recv.at[n],
            device_id=device,
            device_id_type=MESH,
        )

    to_above = [
        layer(0, field.at[0, cx - 1], halo_first.at[0], above),
        layer(1, field.at[1, cx - 1], halo_first.at[1], above),
    ]
    to_below = [layer(2, field.at[0, 0], halo_first.at[2], below)]
    after, ahead = {"own": o + 1}, {"own": o - 1}
    to_after = [
        layer(3, field.at[0, :, pl.ds(cy - 1, 1)], halo_second.at[0], after),
        layer(4, field.at[2, :, pl.ds(cy - 1, 1)], halo_second.at[1], after),
    ]
    to_ahead = [layer(5, field.at[0, :, pl.ds(0, 1)], halo_second.at[2], ahead)]

    def start(copies):
        for copy in copies:
            copy.start()

    def wait_recv(copies):
        for copy in copies:
            copy.wait_recv()

    def wait_send(copies):
        for copy in copies:
            copy.wait_send()

    has_after, has_ahead = o < owners - 1, o > 0
    has_above, has_below = g < groups - 1, g > 0

    for copy in mesh_in:
        copy.wait()
    neighbours = (g + groups - 1) // groups + (2 * groups - 2 - g) // groups
    pl.semaphore_wait(barrier, owners - 1 + neighbours)
    for k in range(owners):
        pl.when(k != me)(lambda k=k: packet(k).start())
    pl.when(has_below)(lambda: start(to_below))
    pl.when(has_above)(lambda: start(to_above))
    pl.when(has_ahead)(lambda: start(to_ahead))
    pl.when(has_after)(lambda: start(to_after))
    landed[pl.ds(me, 1)] = packed[pl.ds(me, 1)]

    pl.when(has_below)(lambda: wait_recv(to_above))
    pl.when(has_above)(lambda: wait_recv(to_below))
    pl.when(has_ahead)(lambda: wait_recv(to_after))
    pl.when(has_after)(lambda: wait_recv(to_ahead))
    model, w1, w2, w3 = field[0], field[1], field[2], field[3]
    shape = (cx, cy, lanes)

    upper = jnp.concatenate([model[1:], halo_first[2][None]], axis=0)
    flux = w1 * (upper - model)
    flux = jnp.where((iota(shape, 0) == cx - 1) & (g == groups - 1), 0.0, flux)
    behind = jnp.where(g == 0, 0.0, halo_first[1] * (model[0] - halo_first[0]))
    smooth = jnp.concatenate([behind[None], flux[:-1]], axis=0) - flux

    row = iota(shape, 1)
    upper = jnp.where(row == cy - 1, halo_second[2], pltpu.roll(model, cy - 1, 1))
    flux = w2 * (upper - model)
    flux = jnp.where((row == cy - 1) & (o == owners - 1), 0.0, flux)
    behind = halo_second[1] * (model[:, 0:1] - halo_second[0])
    behind = jnp.where(o == 0, 0.0, behind)
    smooth = smooth + (jnp.where(row == 0, behind, pltpu.roll(flux, 1, 1)) - flux)

    cell = iota(shape, 2)
    flux = jnp.where(cell == lanes - 1, 0.0, w3 * (pltpu.roll(model, lanes - 1, 2) - model))
    smooth = smooth + (jnp.where(cell == 0, 0.0, pltpu.roll(flux, 1, 2)) - flux)

    cells = cx * cy
    total = jnp.zeros((cells, 2 * lanes), F32)
    for q in range(0, owners, per_row):

        def arrive(count, q=q):
            pltpu.make_async_remote_copy(
                src_ref=packed.at[pl.ds(q, count), pl.ds(0, CAP + 1)],
                dst_ref=landed.at[pl.ds(q, count), pl.ds(0, CAP + 1)],
                send_sem=send_sem.at[0],
                recv_sem=recv_sem.at[q // per_row],
                device_id=peers[0],
                device_id_type=MESH,
            ).wait_recv()

        mine = me // per_row == q // per_row
        pl.when(mine)(lambda: arrive(per_row - 1))
        pl.when(jnp.logical_not(mine))(lambda: arrive(per_row))
        name = landed[q, CAP : CAP + 1]
        for k in range(q + 1, q + per_row):
            name = name + landed[k, CAP : CAP + 1]
        hit = jnp.where(iota((cells, lanes), 0) == name.astype(jnp.int32), 1.0, 0.0).astype(BF16)
        got = landed[pl.ds(q, per_row), pl.ds(0, CAP)].reshape(lanes, lanes)
        total = total + jnp.dot(hit, split(got), preferred_element_type=F32)
    data = (total[:, :lanes] + total[:, lanes:]).reshape(shape)
    out_ref[...] = data + smooth

    packet(0, owners - 1).wait_send()
    pl.when(has_above)(lambda: wait_send(to_above))
    pl.when(has_below)(lambda: wait_send(to_below))
    pl.when(has_after)(lambda: wait_send(to_after))
    pl.when(has_ahead)(lambda: wait_send(to_ahead))


def solution(mesh):
    groups, owners = mesh.shape["grp"], mesh.shape["own"]
    xs = 4
    ys = owners // xs

    def per_device(sens, res, model, first, second, depth, sounding, owner, column, live):
        blocks, nd, lanes = sens.shape
        cx, cy, _ = model.shape
        chunks = 8
        hbm = pl.BlockSpec(memory_space=pltpu.HBM)
        return pl.pallas_call(
            functools.partial(kernel, groups, xs, ys, chunks),
            out_shape=pltpu.VMEM(model.shape, F32),
            in_specs=[hbm] * 10,
            out_specs=pl.BlockSpec(memory_space=pltpu.VMEM),
            scratch_shapes=[
                pltpu.VMEM((blocks * nd, lanes), BF16),
                pltpu.VMEM(res.shape, BF16),
                pltpu.VMEM((4, cx, cy, lanes), F32),
                pltpu.VMEM((3, 1, blocks), jnp.int32),
                pltpu.SMEM((1,), jnp.int32),
                pltpu.VMEM((blocks, 2 * lanes), BF16),
                pltpu.VMEM((owners, CAP + 8, lanes), F32),
                pltpu.VMEM((owners, CAP + 8, lanes), F32),
                pltpu.VMEM((3, cy, lanes), F32),
                pltpu.VMEM((3, cx, 1, lanes), F32),
                pltpu.SemaphoreType.DMA((chunks,)),
                pltpu.SemaphoreType.DMA((9,)),
                pltpu.SemaphoreType.DMA((1,)),
                pltpu.SemaphoreType.DMA((owners // (lanes // CAP),)),
                pltpu.SemaphoreType.DMA((6,)),
                pltpu.SemaphoreType.DMA((6,)),
            ],
            compiler_params=pltpu.CompilerParams(
                collective_id=0, has_side_effects=True, vmem_limit_bytes=60 * 1024 * 1024
            ),
        )(
            sens.reshape(blocks * nd, lanes),
            res,
            model,
            first,
            second,
            depth,
            sounding.reshape(1, blocks),
            owner.reshape(1, blocks),
            column.reshape(1, blocks),
            live,
        )

    both = ("grp", "own")
    mesh_spec = P("grp", "own", None)
    return jax.shard_map(
        per_device,
        mesh=mesh,
        in_specs=(
            P(both, None, None),
            P(both, None),
            mesh_spec,
            mesh_spec,
            mesh_spec,
            mesh_spec,
            P(both),
            P(both, None),
            P(both),
            P(both),
        ),
        out_specs=mesh_spec,
        check_vma=False,
    )
```

```python
import functools

import jax
import jax.numpy as jnp
from jax import lax
from jax.experimental import pallas as pl
from jax.experimental.pallas import tpu as pltpu
from jax.sharding import PartitionSpec as P

MESH = pl.DeviceIdType.MESH
CAP = 16
F32 = jnp.float32
BF16 = jnp.bfloat16


def iota(shape, dim):
    return lax.broadcasted_iota(jnp.int32, shape, dim)


def rings(count):
    return sorted(range(count), key=lambda d: (min(d, count - d), d))


def split(values):
    high = values.astype(BF16)
    low = (values - high.astype(F32)).astype(BF16)
    return jnp.concatenate([high, low], axis=-1)


def kernel(
    groups,
    xs,
    ys,
    chunks,
    sens_hbm,
    res_hbm,
    model_hbm,
    first_hbm,
    second_hbm,
    depth_hbm,
    sounding_hbm,
    owner_hbm,
    column_hbm,
    live_hbm,
    out_ref,
    sens,
    res,
    field,
    index,
    live,
    terms,
    packed,
    landed,
    halo_first,
    halo_second,
    sens_sem,
    in_sem,
    send_sem,
    recv_sem,
    halo_send,
    halo_recv,
    entered,
    spots,
):
    owners = xs * ys
    g = lax.axis_index("grp")
    o = lax.axis_index("own")
    x, y = o // ys, o % ys
    blocks = index.shape[2]
    nd = sens.shape[0] // blocks
    lanes = sens.shape[1]
    order = rings(ys)
    far = y // (ys // 2 + 1)
    me = ((1 - far) * (2 * y - (y + ys - 1) // ys) + far * 2 * (ys - y)) * xs + x

    small = [
        pltpu.make_async_copy(owner_hbm, index.at[0], in_sem.at[0]),
        pltpu.make_async_copy(column_hbm, index.at[1], in_sem.at[1]),
        pltpu.make_async_copy(sounding_hbm, index.at[2], in_sem.at[2]),
        pltpu.make_async_copy(live_hbm, live, in_sem.at[3]),
        pltpu.make_async_copy(res_hbm, res, in_sem.at[4]),
    ]
    for copy in small:
        copy.start()
    rows = sens.shape[0] // chunks
    big = [
        pltpu.make_async_copy(
            sens_hbm.at[pl.ds(c * rows, rows)], sens.at[pl.ds(c * rows, rows)], sens_sem.at[c]
        )
        for c in range(chunks)
    ]
    for copy in big:
        copy.start()
    mesh_in = [
        pltpu.make_async_copy(src, field.at[k], in_sem.at[5 + k])
        for k, src in enumerate((model_hbm, first_hbm, second_hbm, depth_hbm))
    ]
    for copy in mesh_in:
        copy.start()

    barrier = pltpu.get_barrier_semaphore()
    below, above = {"grp": g - 1}, {"grp": g + 1}
    has_after, has_ahead = o < owners - 1, o > 0
    has_above, has_below = g < groups - 1, g > 0
    turn = me // xs
    sides = sorted(range(1, xs), key=lambda d: min(d, xs - d))

    def device(px, py):
        return {"own": px * ys + py}

    def tell(semaphore, to):
        pl.semaphore_signal(semaphore, inc=1, device_id=to, device_id_type=MESH)

    late_from = 3
    late = turn >= late_from
    early = turn < late_from
    for dx in sides:
        tell(barrier, device((x + dx) % xs, y))
    for p in range(ys):

        def greet(p=p):
            tell(barrier, device(x, order[p]))
            if p >= late_from:
                for dx in sides:
                    tell(barrier, device((x + dx) % xs, order[p]))

        pl.when(p != turn)(greet)
    pl.when(has_above)(lambda: tell(barrier, above))
    with_below = (g + groups - 1) // groups

    def meet_all():
        pl.semaphore_wait(barrier, owners - 1 + with_below)
        pl.when(has_below)(lambda: tell(entered.at[0], below))

    def meet():
        pl.semaphore_wait(barrier, xs - 1 + ys - 1 + with_below)
        for dx in sides:
            tell(entered.at[xs - dx], device((x + dx) % xs, y))
        pl.when(has_below)(lambda: tell(entered.at[0], below))

    for copy in small[:4]:
        copy.wait()
    owner = index[0]
    column = index[1]
    sounding = index[2]
    row = owner % ys
    row = jnp.where(row > ys // 2, 2 * (ys - row), jnp.maximum(2 * row - 1, 0))
    target = row * xs + owner // ys
    hot = jnp.where(iota((owners, blocks), 0) == target, 1.0, 0.0)
    before = jnp.where(iota((blocks, blocks), 0) < iota((blocks, blocks), 1), 1.0, 0.0)
    earlier = jnp.dot(hot.astype(BF16), before.astype(BF16), preferred_element_type=F32)
    rank = jnp.sum(hot * earlier, axis=0, keepdims=True).astype(jnp.int32)
    slot = target * CAP + rank

    value = jnp.where(
        lax.rem(iota((lanes, blocks), 0), CAP) == rank, column.astype(F32), 0.0
    )
    tag = lax.dot_general(
        hot.astype(BF16),
        value.astype(BF16),
        (((1,), (1,)), ((), ())),
        preferred_element_type=F32,
    )
    per_row = lanes // CAP
    tag = jnp.where(iota((owners, lanes), 1) // CAP == me % per_row, tag, 0.0)
    for k in range(owners):
        packed[k, CAP : CAP + 1] = tag[k : k + 1]

    at_once = owners // 4
    for k in range(0, owners, at_once):
        spots[pl.ds(k * CAP, at_once * CAP)] = jnp.where(
            iota((at_once * CAP, blocks), 0) + k * CAP == slot, 1.0, 0.0
        ).astype(BF16)

    small[4].wait()
    keep = iota((1, blocks), 1) < live[0]
    picked = jnp.where(
        (iota((res.shape[0], blocks), 0) == sounding) & keep, 1.0, 0.0
    ).astype(BF16)
    twice = jnp.concatenate([res[...]] * (lanes // nd), axis=1)
    chosen = lax.dot_general(
        picked, twice, (((0,), (0,)), ((), ())), preferred_element_type=F32
    ).astype(BF16)
    at_once = 16
    wide = at_once * nd
    diagonal = jnp.where(
        iota((at_once, wide), 0) == iota((at_once, wide), 1) // nd, 1.0, 0.0
    ).astype(BF16)
    done = 0
    for b in range(0, blocks, at_once):
        while done * rows < (b + at_once) * nd:
            big[done].wait()
            done += 1
        left = jnp.concatenate([chosen[b : b + at_once]] * (wide // lanes), axis=1) * diagonal
        part = jnp.dot(left, sens[pl.ds(b * nd, wide)], preferred_element_type=F32)
        terms[pl.ds(b, at_once)] = split(part)

    step = owners // 4
    for k in range(0, owners, step):
        both = jnp.dot(spots[pl.ds(k * CAP, step * CAP)], terms[...], preferred_element_type=F32)
        sums = (both[:, :lanes] + both[:, lanes:]).reshape(step, CAP, lanes)
        packed[pl.ds(k, step), pl.ds(0, CAP)] = sums

    def packet(px, p):
        return pltpu.make_async_remote_copy(
            src_ref=packed.at[pl.ds(p * xs + px, 1), pl.ds(0, CAP + 1)],
            dst_ref=landed.at[pl.ds(me, 1), pl.ds(0, CAP + 1)],
            send_sem=send_sem.at[0],
            recv_sem=recv_sem.at[me // per_row],
            device_id=device(px, order[p]),
            device_id_type=MESH,
        )

    cx, cy = field.shape[1], field.shape[2]

    def layer(n, src, dst, to):
        return pltpu.make_async_remote_copy(
            src_ref=src,
            dst_ref=dst,
            send_sem=halo_send.at[n],
            recv_sem=halo_recv.at[n],
            device_id=to,
            device_id_type=MESH,
        )

    to_above = [
        layer(0, field.at[0, cx - 1], halo_first.at[0], above),
        layer(1, field.at[1, cx - 1], halo_first.at[1], above),
    ]
    to_below = [layer(2, field.at[0, 0], halo_first.at[2], below)]
    after, ahead = {"own": o + 1}, {"own": o - 1}
    to_after = [
        layer(3, field.at[0, :, pl.ds(cy - 1, 1)], halo_second.at[0], after),
        layer(4, field.at[2, :, pl.ds(cy - 1, 1)], halo_second.at[1], after),
    ]
    to_ahead = [layer(5, field.at[0, :, pl.ds(0, 1)], halo_second.at[2], ahead)]

    def start(copies):
        for copy in copies:
            copy.start()

    def wait_recv(copies):
        for copy in copies:
            copy.wait_recv()

    def wait_send(copies):
        for copy in copies:
            copy.wait_send()

    for copy in mesh_in:
        copy.wait()
    pl.when(early)(meet)
    pl.when(late)(meet_all)

    def send_column(px):
        for p in [0, 2, 3, 1, 4, 5, 6, 7]:
            pl.when(p != turn)(lambda p=p: packet(px, p).start())

    def send_row(p):
        for dx in sides:
            packet((x + dx) % xs, p).start()

    def send_late():
        for p in [0, 2, 3, 1, 4, 5, 6, 7]:
            for px in range(xs):
                pl.when((p != turn) | (px != x))(lambda p=p, px=px: packet(px, p).start())

    def send_early():
        send_column(x)
        for p in range(late_from):
            pl.when(p == turn)(functools.partial(send_row, p))

    pl.when(late)(send_late)
    pl.when(early)(send_early)
    pl.when(has_below)(lambda: start(to_below))
    pl.when(y > 0)(lambda: start(to_ahead))
    pl.when(y < ys - 1)(lambda: start(to_after))

    def send_rest():
        for px in range(xs):

            def column_at(px=px):
                pl.semaphore_wait(entered.at[(px - x + xs) % xs], 1)
                send_column(px)

            pl.when(px != x)(column_at)

    pl.when(early)(send_rest)
    pl.when(has_ahead & (y == 0))(lambda: start(to_ahead))
    pl.when(has_after & (y == ys - 1))(lambda: start(to_after))

    def tell_above():
        pl.semaphore_wait(entered.at[0], 1)
        start(to_above)

    pl.when(has_above)(tell_above)
    landed[pl.ds(me, 1)] = packed[pl.ds(me, 1)]

    pl.when(has_below)(lambda: wait_recv(to_above))
    pl.when(has_above)(lambda: wait_recv(to_below))
    pl.when(has_ahead)(lambda: wait_recv(to_after))
    pl.when(has_after)(lambda: wait_recv(to_ahead))
    model, w1, w2, w3 = field[0], field[1], field[2], field[3]
    shape = (cx, cy, lanes)

    upper = jnp.concatenate([model[1:], halo_first[2][None]], axis=0)
    flux = w1 * (upper - model)
    flux = jnp.where((iota(shape, 0) == cx - 1) & (g == groups - 1), 0.0, flux)
    behind = jnp.where(g == 0, 0.0, halo_first[1] * (model[0] - halo_first[0]))
    smooth = jnp.concatenate([behind[None], flux[:-1]], axis=0) - flux

    row = iota(shape, 1)
    upper = jnp.where(row == cy - 1, halo_second[2], pltpu.roll(model, cy - 1, 1))
    flux = w2 * (upper - model)
    flux = jnp.where((row == cy - 1) & (o == owners - 1), 0.0, flux)
    behind = halo_second[1] * (model[:, 0:1] - halo_second[0])
    behind = jnp.where(o == 0, 0.0, behind)
    smooth = smooth + (jnp.where(row == 0, behind, pltpu.roll(flux, 1, 1)) - flux)

    cell = iota(shape, 2)
    flux = jnp.where(cell == lanes - 1, 0.0, w3 * (pltpu.roll(model, lanes - 1, 2) - model))
    smooth = smooth + (jnp.where(cell == 0, 0.0, pltpu.roll(flux, 1, 2)) - flux)

    cells = cx * cy
    total = jnp.zeros((cells, 2 * lanes), F32)
    for q in range(0, owners, per_row):

        def arrive(count, q=q):
            pltpu.make_async_remote_copy(
                src_ref=packed.at[pl.ds(q, count), pl.ds(0, CAP + 1)],
                dst_ref=landed.at[pl.ds(q, count), pl.ds(0, CAP + 1)],
                send_sem=send_sem.at[0],
                recv_sem=recv_sem.at[q // per_row],
                device_id=after,
                device_id_type=MESH,
            ).wait_recv()

        mine = me // per_row == q // per_row
        pl.when(mine)(lambda: arrive(per_row - 1))
        pl.when(jnp.logical_not(mine))(lambda: arrive(per_row))
        name = landed[q, CAP : CAP + 1]
        for k in range(q + 1, q + per_row):
            name = name + landed[k, CAP : CAP + 1]
        hit = jnp.where(iota((cells, lanes), 0) == name.astype(jnp.int32), 1.0, 0.0).astype(BF16)
        got = landed[pl.ds(q, per_row), pl.ds(0, CAP)].reshape(lanes, lanes)
        total = total + jnp.dot(hit, split(got), preferred_element_type=F32)
    data = (total[:, :lanes] + total[:, lanes:]).reshape(shape)
    out_ref[...] = data + smooth

    pltpu.make_async_remote_copy(
        src_ref=packed.at[pl.ds(0, owners - 1), pl.ds(0, CAP + 1)],
        dst_ref=landed.at[pl.ds(0, owners - 1), pl.ds(0, CAP + 1)],
        send_sem=send_sem.at[0],
        recv_sem=recv_sem.at[0],
        device_id=after,
        device_id_type=MESH,
    ).wait_send()
    pl.when(has_above)(lambda: wait_send(to_above))
    pl.when(has_below)(lambda: wait_send(to_below))
    pl.when(has_after)(lambda: wait_send(to_after))
    pl.when(has_ahead)(lambda: wait_send(to_ahead))


def solution(mesh):
    groups, owners = mesh.shape["grp"], mesh.shape["own"]
    xs = 4
    ys = owners // xs

    def per_device(sens, res, model, first, second, depth, sounding, owner, column, live):
        blocks, nd, lanes = sens.shape
        cx, cy, _ = model.shape
        chunks = 4
        hbm = pl.BlockSpec(memory_space=pltpu.HBM)
        return pl.pallas_call(
            functools.partial(kernel, groups, xs, ys, chunks),
            out_shape=pltpu.VMEM(model.shape, F32),
            in_specs=[hbm] * 10,
            out_specs=pl.BlockSpec(memory_space=pltpu.VMEM),
            scratch_shapes=[
                pltpu.VMEM((blocks * nd, lanes), BF16),
                pltpu.VMEM(res.shape, BF16),
                pltpu.VMEM((4, cx, cy, lanes), F32),
                pltpu.VMEM((3, 1, blocks), jnp.int32),
                pltpu.SMEM((1,), jnp.int32),
                pltpu.VMEM((blocks, 2 * lanes), BF16),
                pltpu.VMEM((owners, CAP + 8, lanes), F32),
                pltpu.VMEM((owners, CAP + 8, lanes), F32),
                pltpu.VMEM((3, cy, lanes), F32),
                pltpu.VMEM((3, cx, 1, lanes), F32),
                pltpu.SemaphoreType.DMA((chunks,)),
                pltpu.SemaphoreType.DMA((9,)),
                pltpu.SemaphoreType.DMA((1,)),
                pltpu.SemaphoreType.DMA((owners // (lanes // CAP),)),
                pltpu.SemaphoreType.DMA((6,)),
                pltpu.SemaphoreType.DMA((6,)),
                pltpu.SemaphoreType.REGULAR((xs,)),
                pltpu.VMEM((owners * CAP, blocks), BF16),
            ],
            compiler_params=pltpu.CompilerParams(
                collective_id=0, has_side_effects=True, vmem_limit_bytes=60 * 1024 * 1024
            ),
        )(
            sens.reshape(blocks * nd, lanes),
            res,
            model,
            first,
            second,
            depth,
            sounding.reshape(1, blocks),
            owner.reshape(1, blocks),
            column.reshape(1, blocks),
            live,
        )

    both = ("grp", "own")
    mesh_spec = P("grp", "own", None)
    return jax.shard_map(
        per_device,
        mesh=mesh,
        in_specs=(
            P(both, None, None),
            P(both, None),
            mesh_spec,
            mesh_spec,
            mesh_spec,
            mesh_spec,
            P(both),
            P(both, None),
            P(both),
            P(both),
        ),
        out_specs=mesh_spec,
        check_vma=False,
    )
```

```python
import functools

import jax
import jax.numpy as jnp
from jax import lax
from jax.experimental import pallas as pl
from jax.experimental.pallas import tpu as pltpu
from jax.sharding import PartitionSpec as P

MESH = pl.DeviceIdType.MESH
CAP = 16
F32 = jnp.float32
BF16 = jnp.bfloat16


def iota(shape, dim):
    return lax.broadcasted_iota(jnp.int32, shape, dim)


def rings(count):
    return sorted(range(count), key=lambda d: (min(d, count - d), d))


def split(values):
    high = values.astype(BF16)
    low = (values - high.astype(F32)).astype(BF16)
    return jnp.concatenate([high, low], axis=-1)


def kernel(
    groups,
    xs,
    ys,
    chunks,
    sens_hbm,
    res_hbm,
    model_hbm,
    first_hbm,
    second_hbm,
    depth_hbm,
    sounding_hbm,
    owner_hbm,
    column_hbm,
    live_hbm,
    out_ref,
    sens,
    res,
    field,
    index,
    live,
    terms,
    packed,
    landed,
    halo_first,
    halo_second,
    sens_sem,
    in_sem,
    send_sem,
    recv_sem,
    halo_send,
    halo_recv,
    entered,
    spots,
):
    owners = xs * ys
    g = lax.axis_index("grp")
    o = lax.axis_index("own")
    x, y = o // ys, o % ys
    blocks = index.shape[2]
    nd = sens.shape[0] // blocks
    lanes = sens.shape[1]
    order = rings(ys)
    far = y // (ys // 2 + 1)
    me = ((1 - far) * (2 * y - (y + ys - 1) // ys) + far * 2 * (ys - y)) * xs + x

    small = [
        pltpu.make_async_copy(owner_hbm, index.at[0], in_sem.at[0]),
        pltpu.make_async_copy(column_hbm, index.at[1], in_sem.at[1]),
        pltpu.make_async_copy(sounding_hbm, index.at[2], in_sem.at[2]),
        pltpu.make_async_copy(live_hbm, live, in_sem.at[3]),
        pltpu.make_async_copy(res_hbm, res, in_sem.at[4]),
    ]
    for copy in small:
        copy.start()
    rows = sens.shape[0] // chunks
    big = [
        pltpu.make_async_copy(
            sens_hbm.at[pl.ds(c * rows, rows)], sens.at[pl.ds(c * rows, rows)], sens_sem.at[c]
        )
        for c in range(chunks)
    ]
    for copy in big:
        copy.start()
    mesh_in = [
        pltpu.make_async_copy(src, field.at[k], in_sem.at[5 + k])
        for k, src in enumerate((model_hbm, first_hbm, second_hbm, depth_hbm))
    ]
    for copy in mesh_in:
        copy.start()

    barrier = pltpu.get_barrier_semaphore()
    below, above = {"grp": g - 1}, {"grp": g + 1}
    has_after, has_ahead = o < owners - 1, o > 0
    has_above, has_below = g < groups - 1, g > 0
    turn = me // xs
    sides = sorted(range(1, xs), key=lambda d: min(d, xs - d))

    def device(px, py):
        return {"own": px * ys + py}

    def tell(semaphore, to):
        pl.semaphore_signal(semaphore, inc=1, device_id=to, device_id_type=MESH)

    late_from = 3
    herald = 2
    first = g == 0
    origin = first & (o == 0)
    late = (turn >= late_from) | (first & (turn == 0))
    early = jnp.logical_not(late)
    with_below = (g + groups - 1) // groups
    is_herald = 1 - ((o - herald) * (o - herald) + owners * owners - 1) // (owners * owners)
    is_origin = 1 - (o + owners - 1) // owners
    without = (1 - with_below) * (1 - is_herald) * (1 - is_origin)

    def greet_row(p):
        for dx in sides:
            tell(barrier, device((x + dx) % xs, order[p]))

    def greet_all():
        for dx in sides:
            tell(barrier, device((x + dx) % xs, y))
        for p in range(ys):

            def greet(p=p):
                tell(barrier, device(x, order[p]))
                if p >= late_from:
                    greet_row(p)
                elif p == 0:
                    pl.when(first)(lambda: greet_row(0))

            pl.when(p != turn)(greet)

    pl.when(jnp.logical_not(origin))(greet_all)
    pl.when(origin)(lambda: tell(barrier, device(0, herald)))
    pl.when(has_above)(lambda: tell(barrier, above))

    def announce():
        for p in range(ys):
            for px in range(xs):
                if px * ys + order[p] not in (0, herald):
                    tell(entered.at[xs], device(px, order[p]))

    def meet_all():
        pl.semaphore_wait(barrier, owners - 1 + with_below - without)
        pl.when(has_below)(lambda: tell(entered.at[0], below))
        pl.when(first & (o == herald))(announce)

    def meet():
        in_column = 1 - (x + xs - 1) // xs
        pl.semaphore_wait(barrier, xs - 1 + ys - 1 + with_below - (1 - with_below) * in_column)
        for dx in sides:
            tell(entered.at[xs - dx], device((x + dx) % xs, y))
        pl.when(has_below)(lambda: tell(entered.at[0], below))

    for copy in small[:4]:
        copy.wait()
    owner = index[0]
    column = index[1]
    sounding = index[2]
    row = owner % ys
    row = jnp.where(row > ys // 2, 2 * (ys - row), jnp.maximum(2 * row - 1, 0))
    target = row * xs + owner // ys
    hot = jnp.where(iota((owners, blocks), 0) == target, 1.0, 0.0)
    before = jnp.where(iota((blocks, blocks), 0) < iota((blocks, blocks), 1), 1.0, 0.0)
    earlier = jnp.dot(hot.astype(BF16), before.astype(BF16), preferred_element_type=F32)
    rank = jnp.sum(hot * earlier, axis=0, keepdims=True).astype(jnp.int32)
    slot = target * CAP + rank

    value = jnp.where(
        lax.rem(iota((lanes, blocks), 0), CAP) == rank, column.astype(F32), 0.0
    )
    tag = lax.dot_general(
        hot.astype(BF16),
        value.astype(BF16),
        (((1,), (1,)), ((), ())),
        preferred_element_type=F32,
    )
    per_row = lanes // CAP
    tag = jnp.where(iota((owners, lanes), 1) // CAP == me % per_row, tag, 0.0)
    for k in range(owners):
        packed[k, CAP : CAP + 1] = tag[k : k + 1]

    at_once = owners // 4
    for k in range(0, owners, at_once):
        spots[pl.ds(k * CAP, at_once * CAP)] = jnp.where(
            iota((at_once * CAP, blocks), 0) + k * CAP == slot, 1.0, 0.0
        ).astype(BF16)

    small[4].wait()
    keep = iota((1, blocks), 1) < live[0]
    picked = jnp.where(
        (iota((res.shape[0], blocks), 0) == sounding) & keep, 1.0, 0.0
    ).astype(BF16)
    twice = jnp.concatenate([res[...]] * (lanes // nd), axis=1)
    chosen = lax.dot_general(
        picked, twice, (((0,), (0,)), ((), ())), preferred_element_type=F32
    ).astype(BF16)
    at_once = 16
    wide = at_once * nd
    diagonal = jnp.where(
        iota((at_once, wide), 0) == iota((at_once, wide), 1) // nd, 1.0, 0.0
    ).astype(BF16)
    done = 0
    for b in range(0, blocks, at_once):
        while done * rows < (b + at_once) * nd:
            big[done].wait()
            done += 1
        left = jnp.concatenate([chosen[b : b + at_once]] * (wide // lanes), axis=1) * diagonal
        part = jnp.dot(left, sens[pl.ds(b * nd, wide)], preferred_element_type=F32)
        terms[pl.ds(b, at_once)] = split(part)

    step = owners // 4
    for k in range(0, owners, step):
        both = jnp.dot(spots[pl.ds(k * CAP, step * CAP)], terms[...], preferred_element_type=F32)
        sums = (both[:, :lanes] + both[:, lanes:]).reshape(step, CAP, lanes)
        packed[pl.ds(k, step), pl.ds(0, CAP)] = sums

    def packet(px, p):
        return pltpu.make_async_remote_copy(
            src_ref=packed.at[pl.ds(p * xs + px, 1), pl.ds(0, CAP + 1)],
            dst_ref=landed.at[pl.ds(me, 1), pl.ds(0, CAP + 1)],
            send_sem=send_sem.at[0],
            recv_sem=recv_sem.at[me // per_row],
            device_id=device(px, order[p]),
            device_id_type=MESH,
        )

    cx, cy = field.shape[1], field.shape[2]

    def layer(n, src, dst, to):
        return pltpu.make_async_remote_copy(
            src_ref=src,
            dst_ref=dst,
            send_sem=halo_send.at[n],
            recv_sem=halo_recv.at[n],
            device_id=to,
            device_id_type=MESH,
        )

    to_above = [
        layer(0, field.at[0, cx - 1], halo_first.at[0], above),
        layer(1, field.at[1, cx - 1], halo_first.at[1], above),
    ]
    to_below = [layer(2, field.at[0, 0], halo_first.at[2], below)]
    after, ahead = {"own": o + 1}, {"own": o - 1}
    to_after = [
        layer(3, field.at[0, :, pl.ds(cy - 1, 1)], halo_second.at[0], after),
        layer(4, field.at[2, :, pl.ds(cy - 1, 1)], halo_second.at[1], after),
    ]
    to_ahead = [layer(5, field.at[0, :, pl.ds(0, 1)], halo_second.at[2], ahead)]

    def start(copies):
        for copy in copies:
            copy.start()

    def wait_recv(copies):
        for copy in copies:
            copy.wait_recv()

    def wait_send(copies):
        for copy in copies:
            copy.wait_send()

    for copy in mesh_in:
        copy.wait()
    pl.when(early)(meet)
    pl.when(late)(meet_all)

    hold = first & (o != herald)
    sequence = [p for p in (0, 2, 3, 1, 4, 5, 6, 7) if p < ys]

    def send_column(px):
        for p in sequence:
            go = p != turn
            if p == 0:
                go = go & jnp.logical_not(hold & (px == 0))
            pl.when(go)(lambda p=p: packet(px, p).start())

    def send_row(p):
        for dx in sides:
            packet((x + dx) % xs, p).start()

    def send_late():
        for p in sequence:
            for px in range(xs):
                go = (p != turn) | (px != x)
                if p == 0 and px == 0:
                    go = go & jnp.logical_not(hold)
                pl.when(go)(lambda p=p, px=px: packet(px, p).start())

    def send_early():
        send_column(x)
        for p in range(late_from):
            pl.when(p == turn)(functools.partial(send_row, p))

    pl.when(late)(send_late)
    pl.when(early)(send_early)
    pl.when(has_below)(lambda: start(to_below))
    pl.when((y > 0) & jnp.logical_not(first & (o == 1)))(lambda: start(to_ahead))
    pl.when(y < ys - 1)(lambda: start(to_after))

    def send_rest():
        for px in range(xs):

            def column_at(px=px):
                pl.semaphore_wait(entered.at[(px - x + xs) % xs], 1)
                send_column(px)

            pl.when(px != x)(column_at)

    pl.when(early)(send_rest)
    pl.when(has_ahead & (y == 0))(lambda: start(to_ahead))
    pl.when(has_after & (y == ys - 1))(lambda: start(to_after))

    def send_origin():
        pl.semaphore_wait(entered.at[xs], 1)
        packet(0, 0).start()
        pl.when(o == 1)(lambda: start(to_ahead))

    pl.when(hold & (o != 0))(send_origin)

    def tell_above():
        pl.semaphore_wait(entered.at[0], 1)
        start(to_above)

    pl.when(has_above)(tell_above)
    landed[pl.ds(me, 1)] = packed[pl.ds(me, 1)]

    pl.when(has_below)(lambda: wait_recv(to_above))
    pl.when(has_above)(lambda: wait_recv(to_below))
    pl.when(has_ahead)(lambda: wait_recv(to_after))
    pl.when(has_after)(lambda: wait_recv(to_ahead))
    model, w1, w2, w3 = field[0], field[1], field[2], field[3]
    shape = (cx, cy, lanes)

    upper = jnp.concatenate([model[1:], halo_first[2][None]], axis=0)
    flux = w1 * (upper - model)
    flux = jnp.where((iota(shape, 0) == cx - 1) & (g == groups - 1), 0.0, flux)
    behind = jnp.where(g == 0, 0.0, halo_first[1] * (model[0] - halo_first[0]))
    smooth = jnp.concatenate([behind[None], flux[:-1]], axis=0) - flux

    row = iota(shape, 1)
    upper = jnp.where(row == cy - 1, halo_second[2], pltpu.roll(model, cy - 1, 1))
    flux = w2 * (upper - model)
    flux = jnp.where((row == cy - 1) & (o == owners - 1), 0.0, flux)
    behind = halo_second[1] * (model[:, 0:1] - halo_second[0])
    behind = jnp.where(o == 0, 0.0, behind)
    smooth = smooth + (jnp.where(row == 0, behind, pltpu.roll(flux, 1, 1)) - flux)

    cell = iota(shape, 2)
    flux = jnp.where(cell == lanes - 1, 0.0, w3 * (pltpu.roll(model, lanes - 1, 2) - model))
    smooth = smooth + (jnp.where(cell == 0, 0.0, pltpu.roll(flux, 1, 2)) - flux)

    cells = cx * cy
    total = jnp.zeros((cells, 2 * lanes), F32)
    for q in range(0, owners, per_row):

        def arrive(count, q=q):
            pltpu.make_async_remote_copy(
                src_ref=packed.at[pl.ds(q, count), pl.ds(0, CAP + 1)],
                dst_ref=landed.at[pl.ds(q, count), pl.ds(0, CAP + 1)],
                send_sem=send_sem.at[0],
                recv_sem=recv_sem.at[q // per_row],
                device_id=after,
                device_id_type=MESH,
            ).wait_recv()

        mine = me // per_row == q // per_row
        pl.when(mine)(lambda: arrive(per_row - 1))
        pl.when(jnp.logical_not(mine))(lambda: arrive(per_row))
        name = landed[q, CAP : CAP + 1]
        for k in range(q + 1, q + per_row):
            name = name + landed[k, CAP : CAP + 1]
        hit = jnp.where(iota((cells, lanes), 0) == name.astype(jnp.int32), 1.0, 0.0).astype(BF16)
        got = landed[pl.ds(q, per_row), pl.ds(0, CAP)].reshape(lanes, lanes)
        total = total + jnp.dot(hit, split(got), preferred_element_type=F32)
    data = (total[:, :lanes] + total[:, lanes:]).reshape(shape)
    out_ref[...] = data + smooth

    pltpu.make_async_remote_copy(
        src_ref=packed.at[pl.ds(0, owners - 1), pl.ds(0, CAP + 1)],
        dst_ref=landed.at[pl.ds(0, owners - 1), pl.ds(0, CAP + 1)],
        send_sem=send_sem.at[0],
        recv_sem=recv_sem.at[0],
        device_id=after,
        device_id_type=MESH,
    ).wait_send()
    pl.when(has_above)(lambda: wait_send(to_above))
    pl.when(has_below)(lambda: wait_send(to_below))
    pl.when(has_after)(lambda: wait_send(to_after))
    pl.when(has_ahead)(lambda: wait_send(to_ahead))


def solution(mesh):
    groups, owners = mesh.shape["grp"], mesh.shape["own"]
    xs = 4
    ys = owners // xs

    def per_device(sens, res, model, first, second, depth, sounding, owner, column, live):
        blocks, nd, lanes = sens.shape
        cx, cy, _ = model.shape
        chunks = 4
        hbm = pl.BlockSpec(memory_space=pltpu.HBM)
        return pl.pallas_call(
            functools.partial(kernel, groups, xs, ys, chunks),
            out_shape=pltpu.VMEM(model.shape, F32),
            in_specs=[hbm] * 10,
            out_specs=pl.BlockSpec(memory_space=pltpu.VMEM),
            scratch_shapes=[
                pltpu.VMEM((blocks * nd, lanes), BF16),
                pltpu.VMEM(res.shape, BF16),
                pltpu.VMEM((4, cx, cy, lanes), F32),
                pltpu.VMEM((3, 1, blocks), jnp.int32),
                pltpu.SMEM((1,), jnp.int32),
                pltpu.VMEM((blocks, 2 * lanes), BF16),
                pltpu.VMEM((owners, CAP + 8, lanes), F32),
                pltpu.VMEM((owners, CAP + 8, lanes), F32),
                pltpu.VMEM((3, cy, lanes), F32),
                pltpu.VMEM((3, cx, 1, lanes), F32),
                pltpu.SemaphoreType.DMA((chunks,)),
                pltpu.SemaphoreType.DMA((9,)),
                pltpu.SemaphoreType.DMA((1,)),
                pltpu.SemaphoreType.DMA((owners // (lanes // CAP),)),
                pltpu.SemaphoreType.DMA((6,)),
                pltpu.SemaphoreType.DMA((6,)),
                pltpu.SemaphoreType.REGULAR((xs + 1,)),
                pltpu.VMEM((owners * CAP, blocks), BF16),
            ],
            compiler_params=pltpu.CompilerParams(
                collective_id=0, has_side_effects=True, vmem_limit_bytes=60 * 1024 * 1024
            ),
        )(
            sens.reshape(blocks * nd, lanes),
            res,
            model,
            first,
            second,
            depth,
            sounding.reshape(1, blocks),
            owner.reshape(1, blocks),
            column.reshape(1, blocks),
            live,
        )

    both = ("grp", "own")
    mesh_spec = P("grp", "own", None)
    return jax.shard_map(
        per_device,
        mesh=mesh,
        in_specs=(
            P(both, None, None),
            P(both, None),
            mesh_spec,
            mesh_spec,
            mesh_spec,
            mesh_spec,
            P(both),
            P(both, None),
            P(both),
            P(both),
        ),
        out_specs=mesh_spec,
        check_vma=False,
    )
```

```python
import functools

import jax
import jax.numpy as jnp
from jax import lax
from jax.experimental import pallas as pl
from jax.experimental.pallas import tpu as pltpu
from jax.sharding import PartitionSpec as P

MESH = pl.DeviceIdType.MESH
CAP = 16
F32 = jnp.float32
BF16 = jnp.bfloat16


def iota(shape, dim):
    return lax.broadcasted_iota(jnp.int32, shape, dim)


def rings(count):
    return sorted(range(count), key=lambda d: (min(d, count - d), d))


def split(values):
    high = values.astype(BF16)
    low = (values - high.astype(F32)).astype(BF16)
    return jnp.concatenate([high, low], axis=-1)


def kernel(
    groups,
    xs,
    ys,
    chunks,
    sens_hbm,
    res_hbm,
    model_hbm,
    first_hbm,
    second_hbm,
    depth_hbm,
    sounding_hbm,
    owner_hbm,
    column_hbm,
    live_hbm,
    out_ref,
    sens,
    res,
    field,
    index,
    live,
    terms,
    packed,
    landed,
    halo_first,
    halo_second,
    sens_sem,
    in_sem,
    send_sem,
    recv_sem,
    halo_send,
    halo_recv,
    entered,
    spots,
):
    owners = xs * ys
    g = lax.axis_index("grp")
    o = lax.axis_index("own")
    x, y = o // ys, o % ys
    blocks = index.shape[2]
    nd = sens.shape[0] // blocks
    lanes = sens.shape[1]
    order = rings(ys)
    far = y // (ys // 2 + 1)
    me = ((1 - far) * (2 * y - (y + ys - 1) // ys) + far * 2 * (ys - y)) * xs + x

    small = [
        pltpu.make_async_copy(owner_hbm, index.at[0], in_sem.at[0]),
        pltpu.make_async_copy(column_hbm, index.at[1], in_sem.at[1]),
        pltpu.make_async_copy(sounding_hbm, index.at[2], in_sem.at[2]),
        pltpu.make_async_copy(live_hbm, live, in_sem.at[3]),
        pltpu.make_async_copy(res_hbm, res, in_sem.at[4]),
    ]
    for copy in small:
        copy.start()
    rows = sens.shape[0] // chunks
    big = [
        pltpu.make_async_copy(
            sens_hbm.at[pl.ds(c * rows, rows)], sens.at[pl.ds(c * rows, rows)], sens_sem.at[c]
        )
        for c in range(chunks)
    ]
    for copy in big:
        copy.start()
    mesh_in = [
        pltpu.make_async_copy(src, field.at[k], in_sem.at[5 + k])
        for k, src in enumerate((model_hbm, first_hbm, second_hbm, depth_hbm))
    ]
    for copy in mesh_in:
        copy.start()

    barrier = pltpu.get_barrier_semaphore()
    below, above = {"grp": g - 1}, {"grp": g + 1}
    has_after, has_ahead = o < owners - 1, o > 0
    has_above, has_below = g < groups - 1, g > 0
    turn = me // xs
    sides = sorted(range(1, xs), key=lambda d: min(d, xs - d))

    def device(px, py):
        return {"own": px * ys + py}

    def tell(semaphore, to):
        pl.semaphore_signal(semaphore, inc=1, device_id=to, device_id_type=MESH)

    late_from = 3
    herald = 2
    first = g == 0
    origin = first & (o == 0)
    late = (turn >= late_from) | (first & (turn == 0))
    early = jnp.logical_not(late)
    with_below = (g + groups - 1) // groups
    is_herald = 1 - ((o - herald) * (o - herald) + owners * owners - 1) // (owners * owners)
    is_origin = 1 - (o + owners - 1) // owners
    without = (1 - with_below) * (1 - is_herald) * (1 - is_origin)

    def greet_row(p):
        for dx in sides:
            tell(barrier, device((x + dx) % xs, order[p]))

    def greet_all():
        for dx in sides:
            tell(barrier, device((x + dx) % xs, y))
        for p in range(ys):

            def greet(p=p):
                tell(barrier, device(x, order[p]))
                if p >= late_from:
                    greet_row(p)
                elif p == 0:
                    pl.when(first)(lambda: greet_row(0))

            pl.when(p != turn)(greet)

    pl.when(jnp.logical_not(origin))(greet_all)
    pl.when(origin)(lambda: tell(barrier, device(0, herald)))
    pl.when(has_above)(lambda: tell(barrier, above))

    def announce():
        for p in range(ys):
            for px in range(xs):
                if px * ys + order[p] not in (0, herald):
                    tell(entered.at[xs], device(px, order[p]))

    def meet_all():
        pl.semaphore_wait(barrier, owners - 1 + with_below - without)
        pl.when(has_below)(lambda: tell(entered.at[0], below))
        pl.when(first & (o == herald))(announce)

    def meet():
        in_column = 1 - (x + xs - 1) // xs
        pl.semaphore_wait(barrier, xs - 1 + ys - 1 + with_below - (1 - with_below) * in_column)
        for dx in sides:
            tell(entered.at[xs - dx], device((x + dx) % xs, y))
        pl.when(has_below)(lambda: tell(entered.at[0], below))

    for copy in small[:4]:
        copy.wait()
    owner = index[0]
    column = index[1]
    sounding = index[2]
    row = owner % ys
    row = jnp.where(row > ys // 2, 2 * (ys - row), jnp.maximum(2 * row - 1, 0))
    target = row * xs + owner // ys
    hot = jnp.where(iota((owners, blocks), 0) == target, 1.0, 0.0)
    before = jnp.where(iota((blocks, blocks), 0) < iota((blocks, blocks), 1), 1.0, 0.0)
    earlier = jnp.dot(hot.astype(BF16), before.astype(BF16), preferred_element_type=F32)
    rank = jnp.sum(hot * earlier, axis=0, keepdims=True).astype(jnp.int32)
    slot = target * CAP + rank

    value = jnp.where(
        lax.rem(iota((lanes, blocks), 0), CAP) == rank, column.astype(F32), 0.0
    )
    tag = lax.dot_general(
        hot.astype(BF16),
        value.astype(BF16),
        (((1,), (1,)), ((), ())),
        preferred_element_type=F32,
    )
    per_row = lanes // CAP
    tag = jnp.where(iota((owners, lanes), 1) // CAP == me % per_row, tag, 0.0)
    for k in range(owners):
        packed[k, CAP : CAP + 1] = tag[k : k + 1]

    at_once = owners // 4
    for k in range(0, owners, at_once):
        spots[pl.ds(k * CAP, at_once * CAP)] = jnp.where(
            iota((at_once * CAP, blocks), 0) + k * CAP == slot, 1.0, 0.0
        ).astype(BF16)

    small[4].wait()
    keep = iota((1, blocks), 1) < live[0]
    picked = jnp.where(
        (iota((res.shape[0], blocks), 0) == sounding) & keep, 1.0, 0.0
    ).astype(BF16)
    twice = jnp.concatenate([res[...]] * (lanes // nd), axis=1)
    chosen = lax.dot_general(
        picked, twice, (((0,), (0,)), ((), ())), preferred_element_type=F32
    ).astype(BF16)
    at_once = 16
    wide = at_once * nd
    diagonal = jnp.where(
        iota((at_once, wide), 0) == iota((at_once, wide), 1) // nd, 1.0, 0.0
    ).astype(BF16)
    done = 0
    for b in range(0, blocks, at_once):
        while done * rows < (b + at_once) * nd:
            big[done].wait()
            done += 1
        left = jnp.concatenate([chosen[b : b + at_once]] * (wide // lanes), axis=1) * diagonal
        part = jnp.dot(left, sens[pl.ds(b * nd, wide)], preferred_element_type=F32)
        terms[pl.ds(b, at_once)] = split(part)

    step = owners // 4
    for k in range(0, owners, step):
        both = jnp.dot(spots[pl.ds(k * CAP, step * CAP)], terms[...], preferred_element_type=F32)
        sums = (both[:, :lanes] + both[:, lanes:]).reshape(step, CAP, lanes)
        packed[pl.ds(k, step), pl.ds(0, CAP)] = sums

    def packet(px, p):
        return pltpu.make_async_remote_copy(
            src_ref=packed.at[pl.ds(p * xs + px, 1), pl.ds(0, CAP + 1)],
            dst_ref=landed.at[pl.ds(me, 1), pl.ds(0, CAP + 1)],
            send_sem=send_sem.at[0],
            recv_sem=recv_sem.at[me // per_row],
            device_id=device(px, order[p]),
            device_id_type=MESH,
        )

    cx, cy = field.shape[1], field.shape[2]

    def layer(n, src, dst, to):
        return pltpu.make_async_remote_copy(
            src_ref=src,
            dst_ref=dst,
            send_sem=halo_send.at[n],
            recv_sem=halo_recv.at[n],
            device_id=to,
            device_id_type=MESH,
        )

    to_above = [
        layer(0, field.at[0, cx - 1], halo_first.at[0], above),
        layer(1, field.at[1, cx - 1], halo_first.at[1], above),
    ]
    to_below = [layer(2, field.at[0, 0], halo_first.at[2], below)]
    after, ahead = {"own": o + 1}, {"own": o - 1}
    to_after = [
        layer(3, field.at[0, :, pl.ds(cy - 1, 1)], halo_second.at[0], after),
        layer(4, field.at[2, :, pl.ds(cy - 1, 1)], halo_second.at[1], after),
    ]
    to_ahead = [layer(5, field.at[0, :, pl.ds(0, 1)], halo_second.at[2], ahead)]

    def start(copies):
        for copy in copies:
            copy.start()

    def wait_recv(copies):
        for copy in copies:
            copy.wait_recv()

    def wait_send(copies):
        for copy in copies:
            copy.wait_send()

    for copy in mesh_in:
        copy.wait()
    pl.when(early)(meet)
    pl.when(late)(meet_all)

    hold = first & (o != herald)
    sequence = [p for p in (0, 2, 3, 1, 4, 5, 6, 7) if p < ys]

    def send_column(px):
        for p in sequence:
            go = p != turn
            if p == 0:
                go = go & jnp.logical_not(hold & (px == 0))
            pl.when(go)(lambda p=p: packet(px, p).start())

    def send_row(p):
        for dx in sides:
            packet((x + dx) % xs, p).start()

    def send_late():
        places = [(px, p) for half in (range(2), range(2, xs)) for p in sequence[:4] for px in half] + [(px, p) for p in sequence[4:] for px in range(xs)]
        for px, p in places:
            go = (p != turn) | (px != x)
            if p == 0 and px == 0:
                go = go & jnp.logical_not(hold)
            pl.when(go)(lambda p=p, px=px: packet(px, p).start())

    def send_early():
        send_column(x)
        for p in range(late_from):
            pl.when(p == turn)(functools.partial(send_row, p))

    pl.when(late)(send_late)
    pl.when(early)(send_early)
    pl.when(has_below)(lambda: start(to_below))
    pl.when((y > 0) & jnp.logical_not(first & (o == 1)))(lambda: start(to_ahead))
    pl.when(y < ys - 1)(lambda: start(to_after))

    def send_rest():
        for px in range(xs):

            def column_at(px=px):
                pl.semaphore_wait(entered.at[(px - x + xs) % xs], 1)
                send_column(px)

            pl.when(px != x)(column_at)

    pl.when(early)(send_rest)
    pl.when(has_ahead & (y == 0))(lambda: start(to_ahead))
    pl.when(has_after & (y == ys - 1))(lambda: start(to_after))

    def send_origin():
        pl.semaphore_wait(entered.at[xs], 1)
        packet(0, 0).start()
        pl.when(o == 1)(lambda: start(to_ahead))

    pl.when(hold & (o != 0))(send_origin)

    def tell_above():
        pl.semaphore_wait(entered.at[0], 1)
        start(to_above)

    pl.when(has_above)(tell_above)
    landed[pl.ds(me, 1)] = packed[pl.ds(me, 1)]

    pl.when(has_below)(lambda: wait_recv(to_above))
    pl.when(has_above)(lambda: wait_recv(to_below))
    pl.when(has_ahead)(lambda: wait_recv(to_after))
    pl.when(has_after)(lambda: wait_recv(to_ahead))
    model, w1, w2, w3 = field[0], field[1], field[2], field[3]
    shape = (cx, cy, lanes)

    upper = jnp.concatenate([model[1:], halo_first[2][None]], axis=0)
    flux = w1 * (upper - model)
    flux = jnp.where((iota(shape, 0) == cx - 1) & (g == groups - 1), 0.0, flux)
    behind = jnp.where(g == 0, 0.0, halo_first[1] * (model[0] - halo_first[0]))
    smooth = jnp.concatenate([behind[None], flux[:-1]], axis=0) - flux

    row = iota(shape, 1)
    upper = jnp.where(row == cy - 1, halo_second[2], pltpu.roll(model, cy - 1, 1))
    flux = w2 * (upper - model)
    flux = jnp.where((row == cy - 1) & (o == owners - 1), 0.0, flux)
    behind = halo_second[1] * (model[:, 0:1] - halo_second[0])
    behind = jnp.where(o == 0, 0.0, behind)
    smooth = smooth + (jnp.where(row == 0, behind, pltpu.roll(flux, 1, 1)) - flux)

    cell = iota(shape, 2)
    flux = jnp.where(cell == lanes - 1, 0.0, w3 * (pltpu.roll(model, lanes - 1, 2) - model))
    smooth = smooth + (jnp.where(cell == 0, 0.0, pltpu.roll(flux, 1, 2)) - flux)

    cells = cx * cy
    total = jnp.zeros((cells, 2 * lanes), F32)
    for q in range(0, owners, per_row):

        def arrive(count, q=q):
            pltpu.make_async_remote_copy(
                src_ref=packed.at[pl.ds(q, count), pl.ds(0, CAP + 1)],
                dst_ref=landed.at[pl.ds(q, count), pl.ds(0, CAP + 1)],
                send_sem=send_sem.at[0],
                recv_sem=recv_sem.at[q // per_row],
                device_id=after,
                device_id_type=MESH,
            ).wait_recv()

        mine = me // per_row == q // per_row
        pl.when(mine)(lambda: arrive(per_row - 1))
        pl.when(jnp.logical_not(mine))(lambda: arrive(per_row))
        name = landed[q, CAP : CAP + 1]
        for k in range(q + 1, q + per_row):
            name = name + landed[k, CAP : CAP + 1]
        hit = jnp.where(iota((cells, lanes), 0) == name.astype(jnp.int32), 1.0, 0.0).astype(BF16)
        got = landed[pl.ds(q, per_row), pl.ds(0, CAP)].reshape(lanes, lanes)
        total = total + jnp.dot(hit, split(got), preferred_element_type=F32)
    data = (total[:, :lanes] + total[:, lanes:]).reshape(shape)
    out_ref[...] = data + smooth

    pltpu.make_async_remote_copy(
        src_ref=packed.at[pl.ds(0, owners - 1), pl.ds(0, CAP + 1)],
        dst_ref=landed.at[pl.ds(0, owners - 1), pl.ds(0, CAP + 1)],
        send_sem=send_sem.at[0],
        recv_sem=recv_sem.at[0],
        device_id=after,
        device_id_type=MESH,
    ).wait_send()
    pl.when(has_above)(lambda: wait_send(to_above))
    pl.when(has_below)(lambda: wait_send(to_below))
    pl.when(has_after)(lambda: wait_send(to_after))
    pl.when(has_ahead)(lambda: wait_send(to_ahead))


def solution(mesh):
    groups, owners = mesh.shape["grp"], mesh.shape["own"]
    xs = 4
    ys = owners // xs

    def per_device(sens, res, model, first, second, depth, sounding, owner, column, live):
        blocks, nd, lanes = sens.shape
        cx, cy, _ = model.shape
        chunks = 4
        hbm = pl.BlockSpec(memory_space=pltpu.HBM)
        return pl.pallas_call(
            functools.partial(kernel, groups, xs, ys, chunks),
            out_shape=pltpu.VMEM(model.shape, F32),
            in_specs=[hbm] * 10,
            out_specs=pl.BlockSpec(memory_space=pltpu.VMEM),
            scratch_shapes=[
                pltpu.VMEM((blocks * nd, lanes), BF16),
                pltpu.VMEM(res.shape, BF16),
                pltpu.VMEM((4, cx, cy, lanes), F32),
                pltpu.VMEM((3, 1, blocks), jnp.int32),
                pltpu.SMEM((1,), jnp.int32),
                pltpu.VMEM((blocks, 2 * lanes), BF16),
                pltpu.VMEM((owners, CAP + 8, lanes), F32),
                pltpu.VMEM((owners, CAP + 8, lanes), F32),
                pltpu.VMEM((3, cy, lanes), F32),
                pltpu.VMEM((3, cx, 1, lanes), F32),
                pltpu.SemaphoreType.DMA((chunks,)),
                pltpu.SemaphoreType.DMA((9,)),
                pltpu.SemaphoreType.DMA((1,)),
                pltpu.SemaphoreType.DMA((owners // (lanes // CAP),)),
                pltpu.SemaphoreType.DMA((6,)),
                pltpu.SemaphoreType.DMA((6,)),
                pltpu.SemaphoreType.REGULAR((xs + 1,)),
                pltpu.VMEM((owners * CAP, blocks), BF16),
            ],
            compiler_params=pltpu.CompilerParams(
                collective_id=0, has_side_effects=True, vmem_limit_bytes=60 * 1024 * 1024
            ),
        )(
            sens.reshape(blocks * nd, lanes),
            res,
            model,
            first,
            second,
            depth,
            sounding.reshape(1, blocks),
            owner.reshape(1, blocks),
            column.reshape(1, blocks),
            live,
        )

    both = ("grp", "own")
    mesh_spec = P("grp", "own", None)
    return jax.shard_map(
        per_device,
        mesh=mesh,
        in_specs=(
            P(both, None, None),
            P(both, None),
            mesh_spec,
            mesh_spec,
            mesh_spec,
            mesh_spec,
            P(both),
            P(both, None),
            P(both),
            P(both),
        ),
        out_specs=mesh_spec,
        check_vma=False,
    )
```

```python
import functools

import jax
import jax.numpy as jnp
from jax import lax
from jax.experimental import pallas as pl
from jax.experimental.pallas import tpu as pltpu
from jax.sharding import PartitionSpec as P

MESH = pl.DeviceIdType.MESH
CAP = 16
F32 = jnp.float32
BF16 = jnp.bfloat16


def iota(shape, dim):
    return lax.broadcasted_iota(jnp.int32, shape, dim)


def rings(count):
    return sorted(range(count), key=lambda d: (min(d, count - d), d))


def split(values):
    high = values.astype(BF16)
    low = (values - high.astype(F32)).astype(BF16)
    return jnp.concatenate([high, low], axis=-1)


def kernel(
    groups,
    xs,
    ys,
    chunks,
    sens_hbm,
    res_hbm,
    model_hbm,
    first_hbm,
    second_hbm,
    depth_hbm,
    sounding_hbm,
    owner_hbm,
    column_hbm,
    live_hbm,
    out_ref,
    sens,
    res,
    field,
    index,
    live,
    terms,
    packed,
    landed,
    halo_first,
    halo_second,
    sens_sem,
    in_sem,
    send_sem,
    recv_sem,
    halo_send,
    halo_recv,
    entered,
    spots,
):
    owners = xs * ys
    g = lax.axis_index("grp")
    o = lax.axis_index("own")
    x, y = o // ys, o % ys
    blocks = index.shape[2]
    nd = sens.shape[0] // blocks
    lanes = sens.shape[1]
    order = rings(ys)
    far = y // (ys // 2 + 1)
    me = ((1 - far) * (2 * y - (y + ys - 1) // ys) + far * 2 * (ys - y)) * xs + x

    small = [
        pltpu.make_async_copy(owner_hbm, index.at[0], in_sem.at[0]),
        pltpu.make_async_copy(column_hbm, index.at[1], in_sem.at[1]),
        pltpu.make_async_copy(sounding_hbm, index.at[2], in_sem.at[2]),
        pltpu.make_async_copy(live_hbm, live, in_sem.at[3]),
        pltpu.make_async_copy(res_hbm, res, in_sem.at[4]),
    ]
    for copy in small:
        copy.start()
    rows = sens.shape[0] // chunks
    big = [
        pltpu.make_async_copy(
            sens_hbm.at[pl.ds(c * rows, rows)], sens.at[pl.ds(c * rows, rows)], sens_sem.at[c]
        )
        for c in range(chunks)
    ]
    for copy in big:
        copy.start()
    mesh_in = [
        pltpu.make_async_copy(src, field.at[k], in_sem.at[5 + k])
        for k, src in enumerate((model_hbm, first_hbm, second_hbm, depth_hbm))
    ]
    for copy in mesh_in:
        copy.start()

    barrier = pltpu.get_barrier_semaphore()
    below, above = {"grp": g - 1}, {"grp": g + 1}
    has_after, has_ahead = o < owners - 1, o > 0
    has_above, has_below = g < groups - 1, g > 0
    turn = me // xs
    sides = sorted(range(1, xs), key=lambda d: min(d, xs - d))

    def device(px, py):
        return {"own": px * ys + py}

    def tell(semaphore, to):
        pl.semaphore_signal(semaphore, inc=1, device_id=to, device_id_type=MESH)

    late_from = 3
    herald = 2
    first = g == 0
    origin = first & (o == 0)
    late = (turn >= late_from) | (first & (turn == 0))
    early = jnp.logical_not(late)
    with_below = (g + groups - 1) // groups
    is_herald = 1 - ((o - herald) * (o - herald) + owners * owners - 1) // (owners * owners)
    is_origin = 1 - (o + owners - 1) // owners
    without = (1 - with_below) * (1 - is_herald) * (1 - is_origin)

    def greet_row(p):
        for dx in sides:
            tell(barrier, device((x + dx) % xs, order[p]))

    def greet_all():
        for dx in sides:
            tell(barrier, device((x + dx) % xs, y))
        for p in range(ys):

            def greet(p=p):
                tell(barrier, device(x, order[p]))
                if p >= late_from:
                    greet_row(p)
                elif p == 0:
                    pl.when(first)(lambda: greet_row(0))

            pl.when(p != turn)(greet)

    pl.when(jnp.logical_not(origin))(greet_all)
    pl.when(origin)(lambda: tell(barrier, device(0, herald)))
    pl.when(has_above)(lambda: tell(barrier, above))

    def announce():
        for p in range(ys):
            for px in range(xs):
                if px * ys + order[p] not in (0, herald):
                    tell(entered.at[xs], device(px, order[p]))

    def meet_all():
        pl.semaphore_wait(barrier, owners - 1 + with_below - without)
        pl.when(has_below)(lambda: tell(entered.at[0], below))
        pl.when(first & (o == herald))(announce)

    def meet():
        in_column = 1 - (x + xs - 1) // xs
        pl.semaphore_wait(barrier, xs - 1 + ys - 1 + with_below - (1 - with_below) * in_column)
        for dx in sides:
            tell(entered.at[xs - dx], device((x + dx) % xs, y))
        pl.when(has_below)(lambda: tell(entered.at[0], below))

    for copy in small[:4]:
        copy.wait()
    owner = index[0]
    column = index[1]
    sounding = index[2]
    row = owner % ys
    row = jnp.where(row > ys // 2, 2 * (ys - row), jnp.maximum(2 * row - 1, 0))
    target = row * xs + owner // ys
    hot = jnp.where(iota((owners, blocks), 0) == target, 1.0, 0.0)
    before = jnp.where(iota((blocks, blocks), 0) < iota((blocks, blocks), 1), 1.0, 0.0)
    earlier = jnp.dot(hot.astype(BF16), before.astype(BF16), preferred_element_type=F32)
    rank = jnp.sum(hot * earlier, axis=0, keepdims=True).astype(jnp.int32)
    slot = target * CAP + rank

    value = jnp.where(
        lax.rem(iota((lanes, blocks), 0), CAP) == rank, column.astype(F32), 0.0
    )
    tag = lax.dot_general(
        hot.astype(BF16),
        value.astype(BF16),
        (((1,), (1,)), ((), ())),
        preferred_element_type=F32,
    )
    per_row = lanes // CAP
    tag = jnp.where(iota((owners, lanes), 1) // CAP == me % per_row, tag, 0.0)
    for k in range(owners):
        packed[k, CAP : CAP + 1] = tag[k : k + 1]

    at_once = owners // 4
    for k in range(0, owners, at_once):
        spots[pl.ds(k * CAP, at_once * CAP)] = jnp.where(
            iota((at_once * CAP, blocks), 0) + k * CAP == slot, 1.0, 0.0
        ).astype(BF16)

    small[4].wait()
    keep = iota((1, blocks), 1) < live[0]
    picked = jnp.where(
        (iota((res.shape[0], blocks), 0) == sounding) & keep, 1.0, 0.0
    ).astype(BF16)
    twice = jnp.concatenate([res[...]] * (lanes // nd), axis=1)
    chosen = lax.dot_general(
        picked, twice, (((0,), (0,)), ((), ())), preferred_element_type=F32
    ).astype(BF16)
    at_once = 16
    wide = at_once * nd
    diagonal = jnp.where(
        iota((at_once, wide), 0) == iota((at_once, wide), 1) // nd, 1.0, 0.0
    ).astype(BF16)
    done = 0
    for b in range(0, blocks, at_once):
        while done * rows < (b + at_once) * nd:
            big[done].wait()
            done += 1
        left = jnp.concatenate([chosen[b : b + at_once]] * (wide // lanes), axis=1) * diagonal
        part = jnp.dot(left, sens[pl.ds(b * nd, wide)], preferred_element_type=F32)
        terms[pl.ds(b, at_once)] = split(part)

    step = owners // 4
    for k in range(0, owners, step):
        both = jnp.dot(spots[pl.ds(k * CAP, step * CAP)], terms[...], preferred_element_type=F32)
        sums = (both[:, :lanes] + both[:, lanes:]).reshape(step, CAP, lanes)
        packed[pl.ds(k, step), pl.ds(0, CAP)] = sums

    def packet(px, p):
        return pltpu.make_async_remote_copy(
            src_ref=packed.at[pl.ds(p * xs + px, 1), pl.ds(0, CAP + 1)],
            dst_ref=landed.at[pl.ds(me, 1), pl.ds(0, CAP + 1)],
            send_sem=send_sem.at[0],
            recv_sem=recv_sem.at[me // per_row],
            device_id=device(px, order[p]),
            device_id_type=MESH,
        )

    cx, cy = field.shape[1], field.shape[2]

    def layer(n, src, dst, to):
        return pltpu.make_async_remote_copy(
            src_ref=src,
            dst_ref=dst,
            send_sem=halo_send.at[n],
            recv_sem=halo_recv.at[n],
            device_id=to,
            device_id_type=MESH,
        )

    to_above = [
        layer(0, field.at[0, cx - 1], halo_first.at[0], above),
        layer(1, field.at[1, cx - 1], halo_first.at[1], above),
    ]
    to_below = [layer(2, field.at[0, 0], halo_first.at[2], below)]
    after, ahead = {"own": o + 1}, {"own": o - 1}
    to_after = [
        layer(3, field.at[0, :, pl.ds(cy - 1, 1)], halo_second.at[0], after),
        layer(4, field.at[2, :, pl.ds(cy - 1, 1)], halo_second.at[1], after),
    ]
    to_ahead = [layer(5, field.at[0, :, pl.ds(0, 1)], halo_second.at[2], ahead)]

    def start(copies):
        for copy in copies:
            copy.start()

    def wait_recv(copies):
        for copy in copies:
            copy.wait_recv()

    def wait_send(copies):
        for copy in copies:
            copy.wait_send()

    for copy in mesh_in:
        copy.wait()
    pl.when(early)(meet)
    pl.when(late)(meet_all)

    hold = first & (o != herald)
    sequence = [p for p in (0, 1, 3, 2, 4, 5, 6, 7) if p < ys]

    def send_column(px):
        for p in sequence:
            go = p != turn
            if p == 0:
                go = go & jnp.logical_not(hold & (px == 0))
            pl.when(go)(lambda p=p: packet(px, p).start())

    def send_row(p):
        for dx in sides:
            packet((x + dx) % xs, p).start()

    def send_late():
        places = [(px, p) for half in (range(2), range(2, xs)) for p in sequence[:4] for px in half] + [(px, p) for p in sequence[4:] for px in range(xs)]
        for px, p in places:
            go = (p != turn) | (px != x)
            if p == 0 and px == 0:
                go = go & jnp.logical_not(hold)
            pl.when(go)(lambda p=p, px=px: packet(px, p).start())

    def send_early():
        send_column(x)
        for p in range(late_from):
            pl.when(p == turn)(functools.partial(send_row, p))

    pl.when(late)(send_late)
    pl.when(early)(send_early)
    pl.when(has_below)(lambda: start(to_below))
    pl.when((y > 0) & jnp.logical_not(first & (o == 1)))(lambda: start(to_ahead))
    pl.when(y < ys - 1)(lambda: start(to_after))

    def send_rest():
        for px in range(xs):

            def column_at(px=px):
                pl.semaphore_wait(entered.at[(px - x + xs) % xs], 1)
                send_column(px)

            pl.when(px != x)(column_at)

    pl.when(early)(send_rest)
    pl.when(has_ahead & (y == 0))(lambda: start(to_ahead))
    pl.when(has_after & (y == ys - 1))(lambda: start(to_after))

    def send_origin():
        pl.semaphore_wait(entered.at[xs], 1)
        packet(0, 0).start()
        pl.when(o == 1)(lambda: start(to_ahead))

    pl.when(hold & (o != 0))(send_origin)

    def tell_above():
        pl.semaphore_wait(entered.at[0], 1)
        start(to_above)

    pl.when(has_above)(tell_above)
    landed[pl.ds(me, 1)] = packed[pl.ds(me, 1)]

    pl.when(has_below)(lambda: wait_recv(to_above))
    pl.when(has_above)(lambda: wait_recv(to_below))
    pl.when(has_ahead)(lambda: wait_recv(to_after))
    pl.when(has_after)(lambda: wait_recv(to_ahead))
    model, w1, w2, w3 = field[0], field[1], field[2], field[3]
    shape = (cx, cy, lanes)

    upper = jnp.concatenate([model[1:], halo_first[2][None]], axis=0)
    flux = w1 * (upper - model)
    flux = jnp.where((iota(shape, 0) == cx - 1) & (g == groups - 1), 0.0, flux)
    behind = jnp.where(g == 0, 0.0, halo_first[1] * (model[0] - halo_first[0]))
    smooth = jnp.concatenate([behind[None], flux[:-1]], axis=0) - flux

    row = iota(shape, 1)
    upper = jnp.where(row == cy - 1, halo_second[2], pltpu.roll(model, cy - 1, 1))
    flux = w2 * (upper - model)
    flux = jnp.where((row == cy - 1) & (o == owners - 1), 0.0, flux)
    behind = halo_second[1] * (model[:, 0:1] - halo_second[0])
    behind = jnp.where(o == 0, 0.0, behind)
    smooth = smooth + (jnp.where(row == 0, behind, pltpu.roll(flux, 1, 1)) - flux)

    cell = iota(shape, 2)
    flux = jnp.where(cell == lanes - 1, 0.0, w3 * (pltpu.roll(model, lanes - 1, 2) - model))
    smooth = smooth + (jnp.where(cell == 0, 0.0, pltpu.roll(flux, 1, 2)) - flux)

    cells = cx * cy
    total = jnp.zeros((cells, 2 * lanes), F32)
    for q in range(0, owners, per_row):

        def arrive(count, q=q):
            pltpu.make_async_remote_copy(
                src_ref=packed.at[pl.ds(q, count), pl.ds(0, CAP + 1)],
                dst_ref=landed.at[pl.ds(q, count), pl.ds(0, CAP + 1)],
                send_sem=send_sem.at[0],
                recv_sem=recv_sem.at[q // per_row],
                device_id=after,
                device_id_type=MESH,
            ).wait_recv()

        mine = me // per_row == q // per_row
        pl.when(mine)(lambda: arrive(per_row - 1))
        pl.when(jnp.logical_not(mine))(lambda: arrive(per_row))
        name = landed[q, CAP : CAP + 1]
        for k in range(q + 1, q + per_row):
            name = name + landed[k, CAP : CAP + 1]
        hit = jnp.where(iota((cells, lanes), 0) == name.astype(jnp.int32), 1.0, 0.0).astype(BF16)
        got = landed[pl.ds(q, per_row), pl.ds(0, CAP)].reshape(lanes, lanes)
        total = total + jnp.dot(hit, split(got), preferred_element_type=F32)
    data = (total[:, :lanes] + total[:, lanes:]).reshape(shape)
    out_ref[...] = data + smooth

    pltpu.make_async_remote_copy(
        src_ref=packed.at[pl.ds(0, owners - 1), pl.ds(0, CAP + 1)],
        dst_ref=landed.at[pl.ds(0, owners - 1), pl.ds(0, CAP + 1)],
        send_sem=send_sem.at[0],
        recv_sem=recv_sem.at[0],
        device_id=after,
        device_id_type=MESH,
    ).wait_send()
    pl.when(has_above)(lambda: wait_send(to_above))
    pl.when(has_below)(lambda: wait_send(to_below))
    pl.when(has_after)(lambda: wait_send(to_after))
    pl.when(has_ahead)(lambda: wait_send(to_ahead))


def solution(mesh):
    groups, owners = mesh.shape["grp"], mesh.shape["own"]
    xs = 4
    ys = owners // xs

    def per_device(sens, res, model, first, second, depth, sounding, owner, column, live):
        blocks, nd, lanes = sens.shape
        cx, cy, _ = model.shape
        chunks = 4
        hbm = pl.BlockSpec(memory_space=pltpu.HBM)
        return pl.pallas_call(
            functools.partial(kernel, groups, xs, ys, chunks),
            out_shape=pltpu.VMEM(model.shape, F32),
            in_specs=[hbm] * 10,
            out_specs=pl.BlockSpec(memory_space=pltpu.VMEM),
            scratch_shapes=[
                pltpu.VMEM((blocks * nd, lanes), BF16),
                pltpu.VMEM(res.shape, BF16),
                pltpu.VMEM((4, cx, cy, lanes), F32),
                pltpu.VMEM((3, 1, blocks), jnp.int32),
                pltpu.SMEM((1,), jnp.int32),
                pltpu.VMEM((blocks, 2 * lanes), BF16),
                pltpu.VMEM((owners, CAP + 8, lanes), F32),
                pltpu.VMEM((owners, CAP + 8, lanes), F32),
                pltpu.VMEM((3, cy, lanes), F32),
                pltpu.VMEM((3, cx, 1, lanes), F32),
                pltpu.SemaphoreType.DMA((chunks,)),
                pltpu.SemaphoreType.DMA((9,)),
                pltpu.SemaphoreType.DMA((1,)),
                pltpu.SemaphoreType.DMA((owners // (lanes // CAP),)),
                pltpu.SemaphoreType.DMA((6,)),
                pltpu.SemaphoreType.DMA((6,)),
                pltpu.SemaphoreType.REGULAR((xs + 1,)),
                pltpu.VMEM((owners * CAP, blocks), BF16),
            ],
            compiler_params=pltpu.CompilerParams(
                collective_id=0, has_side_effects=True, vmem_limit_bytes=60 * 1024 * 1024
            ),
        )(
            sens.reshape(blocks * nd, lanes),
            res,
            model,
            first,
            second,
            depth,
            sounding.reshape(1, blocks),
            owner.reshape(1, blocks),
            column.reshape(1, blocks),
            live,
        )

    both = ("grp", "own")
    mesh_spec = P("grp", "own", None)
    return jax.shard_map(
        per_device,
        mesh=mesh,
        in_specs=(
            P(both, None, None),
            P(both, None),
            mesh_spec,
            mesh_spec,
            mesh_spec,
            mesh_spec,
            P(both),
            P(both, None),
            P(both),
            P(both),
        ),
        out_specs=mesh_spec,
        check_vma=False,
    )
```
